32 devices in a mesh: dp: 8 (over z, y), hid: 4 (over x, core).
Axes of the slice: x: 2, y: 2, z: 4, core: 2. Of those that a mesh axis runs over, the one named last changes fastest.
Arguments:
- gate_pre: bfloat16 [1024, 2, 8192], P('dp', None, 'hid'), may hold values from -6 to 6
- up_pre: bfloat16 [1024, 2, 8192], P('dp', None, 'hid'), may hold values from -6 to 6
- out_grad: bfloat16 [1024, 6144], P('dp'), may hold values from -6 to 6
- combine: float32 [1024, 2], P('dp'), may hold values from 0.1 to 0.9
- expert_ids: int32 [1024, 2], P('dp'), may hold values from 0 to 7, all different within a row; in each aligned block of 128 rows (0 to 127, 128 to 255, ...) at most 48 rows name the same one
- down_weight: bfloat16 [8, 8192, 6144], P('dp', 'hid'), may hold values from -0.0625 to 0.0625
Outputs:
- mixed: bfloat16 [1024, 1, 6144], P('dp', None, 'hid')
- combine_grad: float32 [1024, 2], P('dp')
- gate_grad: bfloat16 [1024, 2, 8192], P('dp', None, 'hid')
- up_grad: bfloat16 [1024, 2, 8192], P('dp', None, 'hid')
- weight_grad: bfloat16 [8, 8192, 6144], P('dp', 'hid')
The draws below stay inside these ranges and needn't reach their ends.
Inputs may be any that keep to these rules, and one draw needn't show every extreme that they name: `expert_ids`: each token names two different experts. Among the 128 tokens of one dp index no expert is named by more than 48 tokens, and in every draw some expert is named by exactly 48 of them.
All inputs are finite; a program needn't handle non-finite values.
Results may differ from the reference program's by a relative error of at most 0.0057.
Values may be sent and summed in bfloat16 or wider, within the bound.
No kernel may reach another device: no remote copies, remote signals or barrier semaphores. Data moves between devices by JAX's collectives and lax.ppermute only.
A program may use at most 448 MiB of HBM per device.

```python
import math
import jax
import jax.numpy as jnp
import numpy as np
from jax import lax

D = 6144
FF = 8192
E = 8
TOP = 2
TOK_DEV = 128
CAP = 48
TOKENS = 1024
SLICES = 1
SLICE = 6144
N_DP = 8


def level_of(own_key, shape, shards, smallest, high):
    def one(axis_at, blocks):
        draws = jax.random.uniform(jax.random.fold_in(jax.random.fold_in(own_key, 6), axis_at), (blocks,), jnp.float32, smallest / len(shards), high / len(shards))
        return jnp.repeat(jnp.exp(draws), shape[axis_at] // blocks).reshape((-1,) + (1,) * (len(shape) - axis_at - 1))

    loudness = one(*shards[0])
    for cut in shards[1:]:
        loudness = loudness * one(*cut)
    return loudness


def deal_out(rng, own, number, rows, count, top, bound, skew):
    order = jax.random.permutation(rng, count)
    packed, usual = shares(count, rows * top, bound, skew, True), shares(count, rows * top, bound, skew, False)
    places = jnp.arange(count)

    def named(lengths, rotation):
        used = int((lengths > 0).sum())
        fixed = max(1, used // 4)
        moved = fixed + (places - fixed + rotation * (used - fixed)) % max(1, count - fixed)
        return jnp.zeros((count,), jnp.int32).at[order[jnp.where(places < fixed, places, moved)]].set(jnp.asarray(lengths, jnp.int32))

    lengths = jnp.where(number % 4 == 0, named(packed, number // 4), named(usual, number - number // 4 - 1))
    mixed = jax.random.permutation(jax.random.fold_in(own, 3), count)
    giver, sink = mixed[0:count // 2 * 2:2], mixed[1:count // 2 * 2:2]
    room = jnp.minimum(lengths[giver] - 1, bound - lengths[sink]) // 2
    room = jnp.where((giver == order[0]) | (sink == order[0]) | (lengths[sink] == 0), 0, jnp.maximum(room, 0))
    moved = jax.random.randint(jax.random.fold_in(own, 4), (count // 2,), 0, 1 << 20) % (room + 1)
    lengths = lengths.at[giver].add(-moved).at[sink].add(moved)
    labels = jnp.searchsorted(jnp.cumsum(lengths), jnp.arange(rows * top), side="right").astype(jnp.int32)
    table = labels.reshape(top, rows).T
    table = table[jax.random.permutation(jax.random.fold_in(own, 1), rows)]
    rotation = jax.random.randint(jax.random.fold_in(own, 2), (rows, 1), 0, top)
    return jnp.take_along_axis(table, (jnp.arange(top)[None, :] + rotation) % top, axis=1)


def shares(count, total, most, slope, full):
    portions = [(1 << 20) // math.isqrt(standing ** slope) + 1 for standing in range(1, count + 1)]
    largest = most if full else min(most, max(-(-total // count), total * portions[0] // sum(portions)))
    least = 1 if total - largest >= count - 1 else 0
    given, rest = [largest] + [least] * (count - 1), total - largest - least * (count - 1)
    while rest > 0:
        free = [i for i in range(1, count) if given[i] < largest] or [i for i in range(1, count) if given[i] < most]
        mass, left = sum([portions[i] for i in free]), rest
        for i in free:
            addition = min(most - given[i], max(1, left * portions[i] // mass), rest)
            given[i] = given[i] + addition
            rest = rest - addition
    return np.array(given)


def centred(stream_key, dims, scale, reach, cuts=(), held_as=jnp.bfloat16):
    array = jax.random.normal(stream_key, dims, jnp.float32) * scale
    if len(cuts) > 0:
        array = level_of(stream_key, dims, cuts, -0.22, 0.18) * array
    return jnp.clip(array, min=-reach, max=reach).astype(held_as)


def setup_inputs(seed: int = 0) -> dict:
    keys = jax.random.split(jax.random.key(seed), 7)
    gate_pre = centred(keys[0], (TOKENS, TOP, FF), 1.0, 6.0, ((0, 8), (2, 4)))
    up_pre = centred(keys[1], (TOKENS, TOP, FF), 1.0, 6.0, ((0, 8), (2, 4)))
    out_grad = centred(keys[2], (TOKENS, D), 1.0, 6.0, ((0, 8),))
    combine = jnp.clip(0.1 + 0.79999997 * jax.random.uniform(keys[3], (TOKENS, TOP), jnp.float32) ** level_of(keys[3], (TOKENS, TOP), ((0, 8),), -0.2, 0.2), 0.1, 0.9)
    expert_ids_keys = jax.random.split(jax.random.fold_in(keys[4], 1), TOKENS // TOK_DEV)
    expert_ids_turns = jax.random.permutation(jax.random.fold_in(keys[4], 3), TOKENS // TOK_DEV)
    expert_ids = jax.vmap(lambda own, number: deal_out(jax.random.fold_in(keys[4], 2), own, number, TOK_DEV, E, TOP, CAP, 2))(expert_ids_keys, expert_ids_turns).reshape((TOKENS, TOP))
    down_weight = centred(keys[5], (E * SLICES, FF, SLICE), FF ** -0.5, 0.0625, ((0, 8), (1, 4)))
    return {"gate_pre": gate_pre, "up_pre": up_pre, "out_grad": out_grad, "combine": combine, "expert_ids": expert_ids, "down_weight": down_weight}


def reference(gate_pre, up_pre, out_grad, combine, expert_ids, down_weight):
    slices = N_DP // E
    slice_width = D // slices
    capacity = CAP
    gate_f = gate_pre.astype(jnp.float32)
    up_f = up_pre.astype(jnp.float32)
    sigmoid_gate = jax.nn.sigmoid(gate_f)
    hidden = (gate_f * sigmoid_gate * up_f).astype(jnp.bfloat16)
    scaled = (combine[:, :, None] * out_grad[:, None, :].astype(jnp.float32)).astype(jnp.bfloat16)
    blocked = expert_ids.reshape(N_DP, TOK_DEV * TOP)
    onehot = (blocked[:, :, None] == jnp.arange(E, dtype=jnp.int32)[None, None, :]).astype(jnp.int32)
    earlier = jnp.cumsum(onehot, axis=1) - onehot
    position = jnp.sum(earlier * onehot, axis=2).astype(jnp.int32)
    device_row = jnp.arange(N_DP, dtype=jnp.int32)[:, None]
    place = ((blocked * N_DP + device_row) * capacity + position).reshape(-1).astype(jnp.int32)
    rows_all = E * N_DP * capacity
    hidden_buf = jnp.zeros((rows_all, FF), jnp.bfloat16).at[place].set(hidden.reshape(-1, FF))
    grad_buf = jnp.zeros((rows_all, D), jnp.bfloat16).at[place].set(scaled.reshape(-1, D))
    hidden_buf = hidden_buf.reshape(E, N_DP * capacity, FF)
    grad_buf = grad_buf.reshape(E, N_DP * capacity, D)
    weights = down_weight.reshape(E, slices, FF, slice_width).transpose(0, 2, 1, 3).reshape(E, FF, D)

    def per_expert(items):
        hid_rows, grad_rows, matrix = items
        outputs = jnp.dot(hid_rows, matrix, preferred_element_type=jnp.float32)
        back = lax.dot_general(grad_rows, matrix, (((1,), (1,)), ((), ())), preferred_element_type=jnp.float32)
        wgrad = lax.dot_general(hid_rows, grad_rows, (((0,), (0,)), ((), ())), preferred_element_type=jnp.float32)
        return outputs, back, wgrad.astype(jnp.bfloat16)

    outputs, backs, wgrads = lax.map(per_expert, (hidden_buf, grad_buf, weights))
    slot_out = outputs.reshape(-1, D)[place].reshape(TOKENS, TOP, D)
    hidden_grad = backs.reshape(-1, FF)[place].reshape(TOKENS, TOP, FF)
    mixed = jnp.sum(combine[:, :, None] * slot_out, axis=1).astype(jnp.bfloat16).reshape(TOKENS, slices, slice_width)
    combine_grad = jnp.sum(out_grad.astype(jnp.float32)[:, None, :] * slot_out, axis=2)
    gate_grad = (hidden_grad * up_f * sigmoid_gate * (1.0 + gate_f * (1.0 - sigmoid_gate))).astype(jnp.bfloat16)
    up_grad = (hidden_grad * gate_f * sigmoid_gate).astype(jnp.bfloat16)
    weight_grad = wgrads.reshape(E, FF, slices, slice_width).transpose(0, 2, 1, 3).reshape(E * slices, FF, slice_width)
    return mixed, combine_grad, gate_grad, up_grad, weight_grad
```

```python
import functools

import jax
import jax.numpy as jnp
from jax import lax
from jax.experimental import pallas as pl
from jax.experimental.pallas import tpu as pltpu
from jax.sharding import PartitionSpec as P

E = 8
TOP = 2
CAP = 48
F32 = jnp.float32
BF16 = jnp.bfloat16
I32 = jnp.int32
PARAMS = pltpu.CompilerParams(vmem_limit_bytes=48 * 1024 * 1024)
TOKEN = jax.ShapeDtypeStruct((8, 128), F32)
ROWS = (((0,), (0,)), ((), ()))
COLUMNS = (((1,), (1,)), ((), ()))
WORK = 1 / 32


def whole(a):
    return pl.BlockSpec(a.shape, lambda *_: (0,) * len(a.shape))


def cost(flops, *arrays):
    size = sum(a.size * jnp.dtype(a.dtype).itemsize for a in arrays)
    return pl.CostEstimate(
        flops=int(flops * WORK), bytes_accessed=int(size * WORK), transcendentals=0
    )


def swap(x, axis, bit, after=()):
    if len(after):
        x = lax.optimization_barrier((x, tuple(after)))[0]
    count = lax.axis_size(axis)
    return lax.ppermute(x, axis, [(i, i ^ bit) for i in range(count)])


def block_table(first, slot_key):
    key = lax.broadcasted_iota(I32, (CAP, slot_key.shape[1]), 0) + first
    return key == slot_key


def table_of(first_ref, slot_key, count):
    return jnp.concatenate(
        [block_table(first_ref[k], slot_key) for k in range(count)], axis=0
    )


def ones(table):
    return jnp.where(table, 1.0, 0.0).astype(BF16)


def stack_blocks(blocks, x_ref):
    at = 0
    for b in blocks:
        x_ref[at : at + b.shape[0], :] = b[...]
        at += b.shape[0]


def scale_kernel(slices, first_ref, slice_ref, hid_ref, ids_ref, weight_ref, *refs):
    grads, o_refs, key_ref = refs[:slices], refs[slices:-1], refs[-1]
    tokens = ids_ref.shape[1]
    slots = tokens * TOP
    count = len(o_refs)
    ids = jnp.concatenate([ids_ref[s : s + 1] for s in range(TOP)], axis=1)
    weight = jnp.concatenate([weight_ref[s : s + 1] for s in range(TOP)], axis=1)
    is_expert = lax.broadcasted_iota(I32, (E, slots), 0) == ids
    before = lax.broadcasted_iota(I32, (slots, slots), 0) < lax.broadcasted_iota(
        I32, (slots, slots), 1
    )
    earlier = jnp.dot(ones(is_expert), ones(before), preferred_element_type=F32)
    place = jnp.sum(jnp.where(is_expert, earlier, 0.0), axis=0, keepdims=True)
    slot_key = ids * CAP + place.astype(I32)
    for s in range(TOP):
        key_ref[s : s + 1, :] = slot_key[:, s * tokens : (s + 1) * tokens]
    table = table_of(first_ref, slot_key, count)
    row_weight = jnp.sum(jnp.where(table, weight, 0.0), axis=1, keepdims=True)
    picks = ones(table[:, :tokens]) + ones(table[:, tokens:])
    picked = [jnp.dot(picks, g[...], preferred_element_type=F32) for g in grads]
    for k, o_ref in enumerate(o_refs):
        at = slice(k * CAP, (k + 1) * CAP)
        rows = picked[0][at]
        for j in range(1, slices):
            rows = jnp.where(slice_ref[k] == j, picked[j][at], rows)
        o_ref[...] = (rows * row_weight[at]).astype(BF16)


def send_scaled(first, dest_slice, my_hid, ids, weight, out_grad, slices, quarter):
    tokens = ids.shape[1]
    hid_count = out_grad.shape[1] // (slices * quarter)
    count = first.shape[0]
    outs = [jax.ShapeDtypeStruct((CAP, quarter), BF16)] * count
    key = jax.ShapeDtypeStruct(ids.shape, I32)

    def part(j):
        return pl.BlockSpec((tokens, quarter), lambda i, f, d, h: (0, j * hid_count + h[0]))

    return pl.pallas_call(
        functools.partial(scale_kernel, slices),
        grid_spec=pltpu.PrefetchScalarGridSpec(
            num_scalar_prefetch=3,
            grid=(1,),
            in_specs=[whole(ids), whole(weight)] + [part(j) for j in range(slices)],
            out_specs=[whole(o) for o in outs] + [whole(key)],
        ),
        out_shape=outs + [key],
        compiler_params=PARAMS,
        cost_estimate=cost(0, *outs, *outs),
        name="send_scaled",
    )(first, dest_slice, my_hid, ids, weight, *[out_grad] * slices)


def hidden_of(gate, up):
    sig = 1.0 / (1.0 + jnp.exp(-gate))
    return sig, (gate * sig * up).astype(BF16)


def send_kernel(first_ref, key_ref, gate_ref, up_ref, *o_refs):
    hidden = hidden_of(gate_ref[...].astype(F32), up_ref[...].astype(F32))[1]
    table = ones(table_of(first_ref, key_ref[...], len(o_refs)))
    rows = jnp.dot(table, hidden, preferred_element_type=F32).astype(BF16)
    for k, o_ref in enumerate(o_refs):
        o_ref[...] = rows[k * CAP : (k + 1) * CAP]


def send_hidden(first, slot_key, gate, up):
    slots, depth = gate.shape
    block = 512
    outs = [jax.ShapeDtypeStruct((CAP, depth), BF16)] * first.shape[0]
    part = pl.BlockSpec((slots, block), lambda i, f: (0, i))
    return pl.pallas_call(
        send_kernel,
        grid_spec=pltpu.PrefetchScalarGridSpec(
            num_scalar_prefetch=1,
            grid=(depth // block,),
            in_specs=[whole(slot_key), part, part],
            out_specs=[pl.BlockSpec((CAP, block), lambda i, f: (0, i)) for _ in outs],
        ),
        out_shape=outs,
        compiler_params=PARAMS,
        cost_estimate=cost(0, gate, up, *outs),
        name="send_hidden",
    )(first, slot_key, gate, up)


def down_kernel(count, added, outs, hid_ref, *refs):
    blocks, w_ref, add_refs = refs[:count], refs[count], refs[count + 1 : count + 1 + added]
    o_refs, x_ref = refs[count + 1 + added : -1], refs[-1]

    @pl.when(pl.program_id(0) == 0)
    def _():
        stack_blocks(blocks, x_ref)

    out = jnp.dot(x_ref[...], w_ref[...], preferred_element_type=F32)
    for a in add_refs:
        out = out + a[...].astype(F32)
    at = 0
    for o_ref in o_refs:
        o_ref[...] = out[at : at + o_ref.shape[0]].astype(o_ref.dtype)
        at += o_ref.shape[0]


def down(my_hid, blocks, weights, q, quarter, dtype, parts=1, add=()):
    depth = blocks[0].shape[1]
    rows = CAP * len(blocks)
    block = min(512, quarter)
    per = quarter // block
    outs = [jax.ShapeDtypeStruct((rows // parts, quarter), dtype)] * parts
    return pl.pallas_call(
        functools.partial(down_kernel, len(blocks), len(add), outs),
        grid_spec=pltpu.PrefetchScalarGridSpec(
            num_scalar_prefetch=1,
            grid=(per,),
            in_specs=[whole(b) for b in blocks]
            + [pl.BlockSpec((depth, block), lambda j, h: (0, (h[0] ^ q) * per + j))]
            + [pl.BlockSpec((rows, block), lambda j, h: (0, j)) for _ in add],
            out_specs=[pl.BlockSpec((rows // parts, block), lambda j, h: (0, j)) for _ in outs],
            scratch_shapes=[pltpu.VMEM((rows, depth), BF16)],
        ),
        out_shape=outs,
        compiler_params=PARAMS,
        cost_estimate=cost(
            2 * rows * depth * quarter, *blocks, *outs, jax.ShapeDtypeStruct((depth, quarter), BF16)
        ),
        name="down",
    )(my_hid, *blocks, weights, *add)


def sum_kernel(a_ref, b_ref, *o_refs):
    for k, o_ref in enumerate(o_refs):
        at = slice(k * CAP, (k + 1) * CAP)
        o_ref[...] = (a_ref[at, :] + b_ref[at, :].astype(F32)).astype(BF16)


def sum_blocks(a, b):
    rows, width = a.shape
    outs = [jax.ShapeDtypeStruct((CAP, width), BF16)] * (rows // CAP)
    return pl.pallas_call(
        sum_kernel,
        grid=(1,),
        in_specs=[whole(a), whole(b)],
        out_specs=[whole(o) for o in outs],
        out_shape=outs,
        compiler_params=PARAMS,
        cost_estimate=cost(0, a, b, *outs),
        name="sum_blocks",
    )(a, b)


def back_kernel(quarter, halves, hid_ref, *refs):
    pieces, w_ref, o_refs, x_ref = refs[:halves], refs[halves], refs[halves + 1 : -1], refs[-1]
    quarters = x_ref.shape[0]

    @pl.when(pl.program_id(0) == 0)
    def _():
        for q in range(quarters):
            per = halves // quarters
            stack_blocks(pieces[q * per : (q + 1) * per], x_ref.at[q])

    total = None
    for q in range(quarters):
        at = pl.multiple_of((hid_ref[0] ^ q) * quarter, 128)
        term = lax.dot_general(
            x_ref[q], w_ref[:, pl.ds(at, quarter)], COLUMNS, preferred_element_type=F32
        )
        total = term if total is None else total + term
    for k, o_ref in enumerate(o_refs):
        o_ref[...] = total[k * CAP : (k + 1) * CAP].astype(BF16)


def back(my_hid, pieces, weights):
    quarter = pieces[0][0].shape[1]
    rows = sum(p.shape[0] for p in pieces[0])
    depth, width = weights.shape
    flat = [p for piece in pieces for p in piece]
    block = 256
    outs = [jax.ShapeDtypeStruct((CAP, depth), BF16)] * (rows // CAP)
    return pl.pallas_call(
        functools.partial(back_kernel, quarter, len(flat)),
        grid_spec=pltpu.PrefetchScalarGridSpec(
            num_scalar_prefetch=1,
            grid=(depth // block,),
            in_specs=[whole(p) for p in flat] + [pl.BlockSpec((block, width), lambda i, h: (i, 0))],
            out_specs=[pl.BlockSpec((CAP, block), lambda i, h: (0, i)) for _ in outs],
            scratch_shapes=[pltpu.VMEM((len(pieces), rows, quarter), BF16)],
        ),
        out_shape=outs,
        compiler_params=PARAMS,
        cost_estimate=cost(2 * rows * depth * width, *flat, weights, *outs),
        name="back",
    )(my_hid, *flat, weights)


def outer_kernel(quarter, count, halves, hid_ref, *refs):
    blocks, pieces = refs[:count], refs[count : count + halves]
    o_ref, done_ref, x_ref, y_ref = refs[count + halves :]
    quarters = y_ref.shape[0]

    @pl.when(pl.program_id(0) == 0)
    def _():
        for q in range(quarters):
            per = halves // quarters
            stack_blocks(pieces[q * per : (q + 1) * per], y_ref.at[q])

    stack_blocks(blocks, x_ref)
    x = x_ref[...]
    for q in range(quarters):
        at = pl.multiple_of((hid_ref[0] ^ q) * quarter, 128)
        o_ref[0, :, pl.ds(at, quarter)] = lax.dot_general(
            x, y_ref[q], ROWS, preferred_element_type=F32
        ).astype(BF16)
    done_ref[...] = jnp.zeros_like(done_ref)


def outer(my_hid, blocks, pieces):
    depth = blocks[0].shape[1]
    rows, quarter = CAP * len(blocks), pieces[0][0].shape[1]
    width = quarter * len(pieces)
    flat = [p for piece in pieces for p in piece]
    block = 512
    out = jax.ShapeDtypeStruct((1, depth, width), BF16)
    return pl.pallas_call(
        functools.partial(outer_kernel, quarter, len(blocks), len(flat)),
        grid_spec=pltpu.PrefetchScalarGridSpec(
            num_scalar_prefetch=1,
            grid=(depth // block,),
            in_specs=[pl.BlockSpec((CAP, block), lambda i, h: (0, i)) for _ in blocks]
            + [whole(p) for p in flat],
            out_specs=[pl.BlockSpec((1, block, width), lambda i, h: (0, i, 0)), whole(TOKEN)],
            scratch_shapes=[
                pltpu.VMEM((rows, block), BF16),
                pltpu.VMEM((len(pieces), rows, quarter), BF16),
            ],
        ),
        out_shape=[out, TOKEN],
        compiler_params=PARAMS,
        cost_estimate=cost(2 * rows * depth * width, *blocks, *flat, out),
        name="outer",
    )(my_hid, *blocks, *flat)


def grads_kernel(count, first_ref, key_ref, gate_ref, up_ref, *refs):
    blocks, dgate_ref, dup_ref, dot_ref, x_ref = refs[:count], *refs[count:]
    stack_blocks(blocks, x_ref)
    table = ones(table_of(first_ref, key_ref[...], count))
    h = lax.dot_general(table, x_ref[...], ROWS, preferred_element_type=F32)
    g, u = gate_ref[...].astype(F32), up_ref[...].astype(F32)
    sig, hidden = hidden_of(g, u)
    dgate_ref[...] = (h * u * sig * (1.0 + g * (1.0 - sig))).astype(BF16)
    dup_ref[...] = (h * g * sig).astype(BF16)
    dots = jnp.sum(hidden.astype(F32) * h, axis=1, keepdims=True)

    @pl.when(pl.program_id(0) == 0)
    def _():
        dot_ref[...] = dots

    @pl.when(pl.program_id(0) > 0)
    def _():
        dot_ref[...] += dots


def grads(first, slot_key, gate, up, blocks):
    slots, depth = gate.shape
    block = 512
    part = pl.BlockSpec((slots, block), lambda i, f: (0, i))
    out = jax.ShapeDtypeStruct(gate.shape, BF16)
    dots = jax.ShapeDtypeStruct((slots, 1), F32)
    return pl.pallas_call(
        functools.partial(grads_kernel, len(blocks)),
        grid_spec=pltpu.PrefetchScalarGridSpec(
            num_scalar_prefetch=1,
            grid=(depth // block,),
            in_specs=[whole(slot_key), part, part]
            + [pl.BlockSpec((CAP, block), lambda i, f: (0, i)) for _ in blocks],
            out_specs=[part, part, whole(dots)],
            scratch_shapes=[pltpu.VMEM((CAP * len(blocks), block), BF16)],
        ),
        out_shape=[out, out, dots],
        compiler_params=PARAMS,
        cost_estimate=cost(0, gate, up, *blocks, out, out),
        name="grads",
    )(first, slot_key, gate, up, *blocks)


def mix_kernel(slices, first_ref, slice_ref, key_ref, weight_ref, *refs):
    blocks, o_ref, x_ref = refs[:-2], refs[-2], refs[-1]
    tokens = key_ref.shape[1]
    stack_blocks(blocks, x_ref)
    x = x_ref[...]
    for j in range(slices):
        rows = []
        for k in range(len(blocks)):
            row = jnp.zeros((CAP, tokens), F32)
            for s in range(TOP):
                hit = block_table(first_ref[k], key_ref[s : s + 1, :])
                row = jnp.where(hit, weight_ref[s : s + 1, :], row)
            rows.append(row if slices == 1 else jnp.where(slice_ref[k] == j, row, 0.0))
        left = jnp.concatenate(rows, axis=0)
        total = None
        for _ in range(3):
            part = left.astype(BF16)
            left = left - part.astype(F32)
            term = lax.dot_general(part, x, ROWS, preferred_element_type=F32)
            total = term if total is None else total + term
        o_ref[j] = total.astype(BF16)


def mixed_of(first, dest_slice, slot_key, weight, blocks, slices):
    tokens = slot_key.shape[1]
    rows, quarter = CAP * len(blocks), blocks[0].shape[1]
    out = jax.ShapeDtypeStruct((slices, tokens, quarter), BF16)
    return pl.pallas_call(
        functools.partial(mix_kernel, slices),
        grid_spec=pltpu.PrefetchScalarGridSpec(
            num_scalar_prefetch=2,
            grid=(1,),
            in_specs=[whole(slot_key), whole(weight)] + [whole(b) for b in blocks],
            out_specs=whole(out),
            scratch_shapes=[pltpu.VMEM((rows, quarter), BF16)],
        ),
        out_shape=out,
        compiler_params=PARAMS,
        cost_estimate=cost(0, *blocks, out),
        name="mixed",
    )(first, dest_slice, slot_key, weight, *blocks)


def per_device(gate_pre, up_pre, out_grad, combine, expert_ids, down_weight):
    dp_count = lax.axis_size("dp")
    hid_count = lax.axis_size("hid")
    my_dp = lax.axis_index("dp").astype(I32)
    my_hid = lax.axis_index("hid").astype(I32).reshape(1)
    slices = dp_count // E
    tokens = gate_pre.shape[0]
    local_ff = gate_pre.shape[2]
    quarter = down_weight.shape[2] // hid_count
    slots = tokens * TOP
    weights = down_weight[0]
    everyone = range(dp_count)

    dest = my_dp ^ jnp.arange(dp_count, dtype=I32)
    first, dest_slice = dest // slices * CAP, dest % slices
    near, far = list(range(dp_count // 2 - 1, 0, -1)), list(range(dp_count - 1, dp_count // 2 - 1, -1))
    low, high = range(dp_count // 2), range(dp_count // 2, dp_count)

    ids, weight = expert_ids.T, combine.T
    *scaled, slot_key = send_scaled(
        first, dest_slice, my_hid, ids, weight, out_grad, slices, quarter
    )
    gate, up = gate_pre.reshape(slots, local_ff), up_pre.reshape(slots, local_ff)
    token_key = slot_key.T.reshape(1, slots)
    hidden = send_hidden(first, token_key, gate, up)

    got_grad = {0: scaled[0]}
    for k in far[:2] + near:
        got_grad[k] = swap(scaled[k], "dp", k)
    for k, ahead in zip(far[2:], near * len(far)):
        got_grad[k] = swap(scaled[k], "dp", k, [got_grad[ahead]])
    half = [
        jnp.concatenate(lax.optimization_barrier(tuple(got_grad[k] for k in part)))
        for part in (low, high)
    ]
    half[0] = lax.optimization_barrier((half[0], hidden))[0]
    got_hidden = {0: hidden[0]}
    for k, j in zip(far, far[2:4] + far[3:4]):
        got_hidden[k] = swap(hidden[k], "dp", k, [got_grad[j]])
    pieces = {0: jnp.concatenate(half)}
    bit = hid_count // 2
    pieces[bit] = jnp.concatenate([swap(h, "hid", bit) for h in half])
    while bit > 1:
        bit //= 2
        for q in sorted(pieces):
            if q ^ bit not in pieces:
                ahead = [got_hidden[k] for k in far[:2]] if q else []
                pieces[q ^ bit] = swap(pieces[q], "hid", bit, ahead)
    got_hidden[near[0]] = swap(hidden[near[0]], "dp", near[0], [pieces[1]])
    for i, k in enumerate(far[3:] + near[1:]):
        got_hidden[k] = swap(hidden[k], "dp", k, [got_hidden[far[min(i, 1)]]])
    pieces = [[pieces[q]] for q in range(hid_count)]
    sent_back = back(my_hid, pieces, weights)
    got_hidden = [got_hidden[k] for k in everyone]
    got_hidden, sent_back = lax.optimization_barrier((got_hidden, sent_back))

    got_back = {0: sent_back[0]}
    for k in far[:2] + near[:1]:
        got_back[k] = swap(sent_back[k], "dp", k)
    sums, parts = {}, {}
    x = got_hidden
    for q in range(hid_count - 1, 0, -2):
        sums[q] = swap(down(my_hid, x, weights, q, quarter, BF16)[0], "hid", 1)
    x = lax.optimization_barrier((x, got_back[far[0]]))[0]
    for q in range(hid_count - 2, 0, -2):
        parts[q] = down(my_hid, x, weights, q, quarter, BF16, 2, [sums[q ^ 1]])
    x = lax.optimization_barrier((x, got_back[far[1]]))[0]
    kept = down(my_hid, x, weights, 0, quarter, F32, 2, [sums[1]])
    for i, k in enumerate(far[2:] + near[1:]):
        got_back[k] = swap(sent_back[k], "dp", k, [got_back[far[min(i, 1)]]])
    got_hidden, _ = lax.optimization_barrier((got_hidden, kept))
    weight_grad, token = outer(my_hid, got_hidden, pieces)
    got_out = {}
    got_back = [got_back[k] for k in everyone]
    for i in (1, 0):
        total = kept[i]
        others = [swap(parts[q][i], "hid", q) for q in sorted(parts)]
        for other in others[1:]:
            total = total + other.astype(F32)
        total = lax.optimization_barrier((total, (token, got_back)))[0]
        blocks = sum_blocks(total, others[0])
        for k, block in zip((low, high)[i], blocks):
            got_out[k] = swap(block, "dp", k) if k else block
    got_out = [got_out[k] for k in everyone]
    got_back, _ = lax.optimization_barrier((got_back, got_out[near[0]]))

    gate_grad, up_grad, dots = grads(first, token_key, gate, up, got_back)
    cg = dots.reshape(tokens, TOP) / combine
    cg = jnp.sum(lax.all_gather(cg, "hid"), axis=0)
    got_out, cg, _ = lax.optimization_barrier((got_out, cg, token))
    mixed = mixed_of(first, dest_slice, slot_key, weight, got_out, slices)
    shape = (tokens, TOP, local_ff)
    return (
        jnp.swapaxes(mixed, 0, 1),
        cg,
        gate_grad.reshape(shape),
        up_grad.reshape(shape),
        weight_grad,
    )


def solution(mesh):
    return jax.shard_map(
        per_device,
        mesh=mesh,
        in_specs=(
            P("dp", None, "hid"),
            P("dp", None, "hid"),
            P("dp", None),
            P("dp", None),
            P("dp", None),
            P("dp", "hid", None),
        ),
        out_specs=(
            P("dp", None, "hid"),
            P("dp", None),
            P("dp", None, "hid"),
            P("dp", None, "hid"),
            P("dp", "hid", None),
        ),
        check_vma=False,
    )
```

```python
import functools

import jax
import jax.numpy as jnp
from jax import lax
from jax.experimental import pallas as pl
from jax.experimental.pallas import tpu as pltpu
from jax.sharding import PartitionSpec as P

E = 8
TOP = 2
CAP = 48
F32 = jnp.float32
BF16 = jnp.bfloat16
I32 = jnp.int32
PARAMS = pltpu.CompilerParams(vmem_limit_bytes=40 * 1024 * 1024)
ROWS = (((0,), (0,)), ((), ()))
COLUMNS = (((1,), (1,)), ((), ()))
WORK = 1 / 1000


def whole(a):
    return pl.BlockSpec(a.shape, lambda *_: (0,) * len(a.shape))


def cost(flops, *arrays):
    size = sum(a.size * jnp.dtype(a.dtype).itemsize for a in arrays)
    return pl.CostEstimate(
        flops=int(flops * WORK), bytes_accessed=int(size * WORK), transcendentals=0
    )


def swap(x, axis, bit, after=()):
    if len(after):
        x = lax.optimization_barrier((x, tuple(after)))[0]
    count = lax.axis_size(axis)
    return lax.ppermute(x, axis, [(i, i ^ bit) for i in range(count)])


def ones(table):
    return jnp.where(table, 1.0, 0.0).astype(BF16)


def block_table(d, slices, slot_key):
    key = lax.broadcasted_iota(I32, (CAP, slot_key.shape[1]), 0) + d // slices * CAP
    return key == slot_key


def table_of(slices, slot_key):
    count = E * slices
    return jnp.concatenate([block_table(d, slices, slot_key) for d in range(count)], axis=0)


def scale_kernel(slices, dp_ref, hid_ref, ids_ref, weight_ref, *refs):
    grads, o_refs, key_ref = refs[:slices], refs[slices:-1], refs[-1]
    tokens = ids_ref.shape[1]
    slots = tokens * TOP
    ids = jnp.concatenate([ids_ref[s : s + 1] for s in range(TOP)], axis=1)
    weight = jnp.concatenate([weight_ref[s : s + 1] for s in range(TOP)], axis=1)
    is_expert = lax.broadcasted_iota(I32, (E, slots), 0) == ids
    before = lax.broadcasted_iota(I32, (slots, slots), 0) < lax.broadcasted_iota(
        I32, (slots, slots), 1
    )
    earlier = jnp.dot(ones(is_expert), ones(before), preferred_element_type=F32)
    place = jnp.sum(jnp.where(is_expert, earlier, 0.0), axis=0, keepdims=True)
    slot_key = ids * CAP + place.astype(I32)
    for s in range(TOP):
        key_ref[s : s + 1, :] = slot_key[:, s * tokens : (s + 1) * tokens]
    to = [dp_ref[0] ^ k for k in range(E * slices)]
    table = jnp.concatenate([block_table(d, slices, slot_key) for d in to], axis=0)
    row_weight = jnp.sum(jnp.where(table, weight, 0.0), axis=1, keepdims=True)
    picks = ones(table[:, :tokens]) + ones(table[:, tokens:])
    picked = [jnp.dot(picks, g[...], preferred_element_type=F32) for g in grads]
    for k, o_ref in enumerate(o_refs):
        at = slice(k * CAP, (k + 1) * CAP)
        rows = picked[0][at]
        for j in range(1, slices):
            rows = jnp.where(to[k] % slices == j, picked[j][at], rows)
        o_ref[...] = (rows * row_weight[at]).astype(BF16)


def send_scaled(my_dp, my_hid, ids, weight, out_grad, slices, quarter):
    tokens = ids.shape[1]
    hid_count = out_grad.shape[1] // (slices * quarter)
    outs = [jax.ShapeDtypeStruct((CAP, quarter), BF16)] * (E * slices)
    key = jax.ShapeDtypeStruct(ids.shape, I32)

    def part(j):
        return pl.BlockSpec((tokens, quarter), lambda i, d, h: (0, j * hid_count + h[0]))

    return pl.pallas_call(
        functools.partial(scale_kernel, slices),
        grid_spec=pltpu.PrefetchScalarGridSpec(
            num_scalar_prefetch=2,
            grid=(1,),
            in_specs=[whole(ids), whole(weight)] + [part(j) for j in range(slices)],
            out_specs=[whole(o) for o in outs] + [whole(key)],
        ),
        out_shape=outs + [key],
        compiler_params=PARAMS,
        cost_estimate=cost(0, *outs),
        name="send_scaled",
    )(my_dp, my_hid, ids, weight, *[out_grad] * slices)


def hidden_of(gate, up):
    sig = 1.0 / (1.0 + jnp.exp(-gate))
    return sig, (gate * sig * up).astype(BF16)


def send_kernel(slices, key_ref, gate_ref, up_ref, o_ref):
    hidden = hidden_of(gate_ref[...].astype(F32), up_ref[...].astype(F32))[1]
    table = ones(table_of(slices, key_ref[...]))
    o_ref[...] = jnp.dot(table, hidden, preferred_element_type=F32).astype(BF16)


def send_hidden(slices, slot_key, gate, up):
    slots, depth = gate.shape
    rows = CAP * E * slices
    block = 512
    out = jax.ShapeDtypeStruct((rows, depth), BF16)
    part = pl.BlockSpec((slots, block), lambda i: (0, i))
    return pl.pallas_call(
        functools.partial(send_kernel, slices),
        grid=(depth // block,),
        in_specs=[whole(slot_key), part, part],
        out_specs=pl.BlockSpec((rows, block), lambda i: (0, i)),
        out_shape=out,
        compiler_params=PARAMS,
        cost_estimate=cost(0, gate, up, out),
        name="send_hidden",
    )(slot_key, gate, up)


def down_kernel(added, hid_ref, x_ref, w_ref, *refs):
    out = jnp.dot(x_ref[...], w_ref[...], preferred_element_type=F32)
    for a in refs[:added]:
        out = out + a[...].astype(F32)
    o_ref = refs[added]
    o_ref[...] = out.astype(o_ref.dtype)


def down(my_hid, x, weights, q, quarter, dtype, *add):
    rows, depth = x.shape
    block = min(512, quarter)
    per = quarter // block
    out = jax.ShapeDtypeStruct((rows, quarter), dtype)
    return pl.pallas_call(
        functools.partial(down_kernel, len(add)),
        grid_spec=pltpu.PrefetchScalarGridSpec(
            num_scalar_prefetch=1,
            grid=(per,),
            in_specs=[
                whole(x),
                pl.BlockSpec((depth, block), lambda j, h: (0, (h[0] ^ q) * per + j)),
            ]
            + [pl.BlockSpec((rows, block), lambda j, h: (0, j)) for _ in add],
            out_specs=pl.BlockSpec((rows, block), lambda j, h: (0, j)),
        ),
        out_shape=out,
        compiler_params=PARAMS,
        cost_estimate=cost(
            2 * rows * depth * quarter, x, out, jax.ShapeDtypeStruct((depth, quarter), BF16)
        ),
        name="down",
    )(my_hid, x, weights, *add)


def sum_kernel(a_ref, b_ref, o_ref):
    o_ref[...] = (a_ref[...] + b_ref[...].astype(F32)).astype(BF16)


def sum_of(a, b):
    rows, width = a.shape
    block = min(512, width)
    part = pl.BlockSpec((rows, block), lambda i: (0, i))
    out = jax.ShapeDtypeStruct((rows, width), BF16)
    return pl.pallas_call(
        sum_kernel,
        grid=(width // block,),
        in_specs=[part, part],
        out_specs=part,
        out_shape=out,
        compiler_params=PARAMS,
        cost_estimate=cost(0, a, b, out),
        name="sum_of",
    )(a, b)


def in_order(dp_ref, halves, y_ref):
    per = halves[0].shape[0] // CAP
    for n, half in enumerate(halves):
        for k in range(per):
            at = pl.multiple_of((dp_ref[0] ^ (n % 2 * per + k)) * CAP, CAP)
            y_ref[n // 2, pl.ds(at, CAP), :] = half[k * CAP : (k + 1) * CAP, :]


def quarter_at(hid_ref, q, quarter):
    return pl.ds(pl.multiple_of((hid_ref[0] ^ q) * quarter, 128), quarter)


def back_kernel(dp_ref, hid_ref, *refs):
    *halves, w_ref, o_ref, y_ref = refs

    @pl.when(pl.program_id(0) == 0)
    def _():
        in_order(dp_ref, halves, y_ref)

    count, _, quarter = y_ref.shape
    total = None
    for q in range(count):
        w = w_ref[:, quarter_at(hid_ref, q, quarter)]
        term = lax.dot_general(y_ref[q], w, COLUMNS, preferred_element_type=F32)
        total = term if total is None else total + term
    o_ref[...] = total.astype(BF16)


def back(my_dp, my_hid, halves, weights):
    rows, quarter = 2 * halves[0].shape[0], halves[0].shape[1]
    depth, width = weights.shape
    block = 256
    out = jax.ShapeDtypeStruct((rows, depth), BF16)
    return pl.pallas_call(
        back_kernel,
        grid_spec=pltpu.PrefetchScalarGridSpec(
            num_scalar_prefetch=2,
            grid=(depth // block,),
            in_specs=[whole(p) for p in halves]
            + [pl.BlockSpec((block, width), lambda i, d, h: (i, 0))],
            out_specs=pl.BlockSpec((rows, block), lambda i, d, h: (0, i)),
            scratch_shapes=[pltpu.VMEM((width // quarter, rows, quarter), BF16)],
        ),
        out_shape=out,
        compiler_params=PARAMS,
        cost_estimate=cost(2 * rows * depth * width, *halves, weights, out),
        name="back",
    )(my_dp, my_hid, *halves, weights)


def outer_kernel(dp_ref, hid_ref, x_ref, *refs):
    *halves, o_ref, y_ref = refs

    @pl.when(pl.program_id(0) == 0)
    def _():
        in_order(dp_ref, halves, y_ref)

    count, _, quarter = y_ref.shape
    x = x_ref[...]
    for q in range(count):
        o_ref[0, :, quarter_at(hid_ref, q, quarter)] = lax.dot_general(
            x, y_ref[q], ROWS, preferred_element_type=F32
        ).astype(BF16)


def outer(my_dp, my_hid, x, halves):
    rows, depth = x.shape
    quarter = halves[0].shape[1]
    width = quarter * len(halves) // 2
    block = 256
    out = jax.ShapeDtypeStruct((1, depth, width), BF16)
    return pl.pallas_call(
        outer_kernel,
        grid_spec=pltpu.PrefetchScalarGridSpec(
            num_scalar_prefetch=2,
            grid=(depth // block,),
            in_specs=[pl.BlockSpec((rows, block), lambda i, d, h: (0, i))]
            + [whole(p) for p in halves],
            out_specs=pl.BlockSpec((1, block, width), lambda i, d, h: (0, i, 0)),
            scratch_shapes=[pltpu.VMEM((width // quarter, rows, quarter), BF16)],
        ),
        out_shape=out,
        compiler_params=PARAMS,
        cost_estimate=cost(2 * rows * depth * width, x, *halves, out),
        name="outer",
    )(my_dp, my_hid, x, *halves)


def grads_kernel(slices, key_ref, gate_ref, up_ref, back_ref, dgate_ref, dup_ref, dot_ref):
    table = ones(table_of(slices, key_ref[...]))
    h = lax.dot_general(table, back_ref[...], ROWS, preferred_element_type=F32)
    g, u = gate_ref[...].astype(F32), up_ref[...].astype(F32)
    sig, hidden = hidden_of(g, u)
    dgate_ref[...] = (h * u * sig * (1.0 + g * (1.0 - sig))).astype(BF16)
    dup_ref[...] = (h * g * sig).astype(BF16)
    dots = jnp.sum(hidden.astype(F32) * h, axis=1, keepdims=True)

    @pl.when(pl.program_id(0) == 0)
    def _():
        dot_ref[...] = dots

    @pl.when(pl.program_id(0) > 0)
    def _():
        dot_ref[...] += dots


def grads(slices, slot_key, gate, up, got_back):
    slots, depth = gate.shape
    rows = got_back.shape[0]
    block = 512
    part = pl.BlockSpec((slots, block), lambda i: (0, i))
    out = jax.ShapeDtypeStruct(gate.shape, BF16)
    dots = jax.ShapeDtypeStruct((slots, 1), F32)
    return pl.pallas_call(
        functools.partial(grads_kernel, slices),
        grid=(depth // block,),
        in_specs=[
            whole(slot_key),
            part,
            part,
            pl.BlockSpec((rows, block), lambda i: (0, i)),
        ],
        out_specs=[part, part, whole(dots)],
        out_shape=[out, out, dots],
        compiler_params=PARAMS,
        cost_estimate=cost(0, gate, up, got_back, out, out),
        name="grads",
    )(slot_key, gate, up, got_back)


def mix_kernel(slices, key_ref, weight_ref, x_ref, *refs):
    o_ref = refs[-1]
    tokens = key_ref.shape[1]
    x = x_ref[...]
    for j in range(slices):
        rows = []
        for d in range(E * slices):
            row = jnp.zeros((CAP, tokens), F32)
            if d % slices == j:
                for s in range(TOP):
                    hit = block_table(d, slices, key_ref[s : s + 1, :])
                    row = jnp.where(hit, weight_ref[s : s + 1, :], row)
            rows.append(row)
        left = jnp.concatenate(rows, axis=0)
        total = None
        for _ in range(3):
            part = left.astype(BF16)
            left = left - part.astype(F32)
            term = lax.dot_general(part, x, ROWS, preferred_element_type=F32)
            total = term if total is None else total + term
        o_ref[j] = total.astype(BF16)


def mixed_of(slices, slot_key, weight, got_out, after):
    tokens = slot_key.shape[1]
    rows, quarter = got_out.shape
    out = jax.ShapeDtypeStruct((slices, tokens, quarter), BF16)
    return pl.pallas_call(
        functools.partial(mix_kernel, slices),
        grid=(1,),
        in_specs=[whole(slot_key), whole(weight), whole(got_out)]
        + [pl.BlockSpec(memory_space=pl.ANY) for _ in after],
        out_specs=whole(out),
        out_shape=out,
        compiler_params=PARAMS,
        cost_estimate=cost(0, got_out, out),
        name="mixed",
    )(slot_key, weight, got_out, *after)


def per_device(gate_pre, up_pre, out_grad, combine, expert_ids, down_weight):
    dp_count = lax.axis_size("dp")
    hid_count = lax.axis_size("hid")
    my_dp = lax.axis_index("dp").astype(I32).reshape(1)
    my_hid = lax.axis_index("hid").astype(I32).reshape(1)
    slices = dp_count // E
    tokens = gate_pre.shape[0]
    local_ff = gate_pre.shape[2]
    quarter = down_weight.shape[2] // hid_count
    slots = tokens * TOP
    weights = down_weight[0]
    ids, weight = expert_ids.T, combine.T

    def over_dp(x):
        return lax.all_to_all(x, "dp", split_axis=0, concat_axis=0, tiled=True)

    *scaled, slot_key = send_scaled(my_dp, my_hid, ids, weight, out_grad, slices, quarter)
    gate, up = gate_pre.reshape(slots, local_ff), up_pre.reshape(slots, local_ff)
    token_key = slot_key.T.reshape(1, slots)
    hidden = send_hidden(slices, token_key, gate, up)

    near, far = range(1, dp_count // 2), range(dp_count // 2, dp_count)
    got = {0: scaled[0]}
    for k in [*near, *far[:2]]:
        got[k] = swap(scaled[k], "dp", k)
    for i, k in enumerate(far[2:]):
        got[k] = swap(scaled[k], "dp", k, [got[near[i % len(near)]]])
    halves = []
    for part in ([0, *near], far):
        blocks = lax.optimization_barrier(tuple(got[k] for k in part))
        piece = {0: jnp.concatenate(blocks)}
        if not halves:
            piece[0], hidden = lax.optimization_barrier((piece[0], hidden))
        bit = hid_count // 2
        while bit:
            for q in sorted(piece):
                piece[q ^ bit] = swap(piece[q], "hid", bit)
            bit //= 2
        halves.append(piece)
    hidden = lax.optimization_barrier((hidden, [got[k] for k in far]))[0]
    got_hidden = over_dp(hidden)
    halves = [piece[q] for q in range(hid_count) for piece in halves]
    sent_back = back(my_dp, my_hid, halves, weights)
    got_hidden, sent_back = lax.optimization_barrier((got_hidden, sent_back))

    got_back = over_dp(sent_back)
    sums = {}
    for q in range(hid_count - 1, 0, -2):
        sums[q] = swap(down(my_hid, got_hidden, weights, q, quarter, BF16), "hid", 1)
    others = []
    for q in range(hid_count - 2, 0, -2):
        made = down(my_hid, got_hidden, weights, q, quarter, BF16, sums[q ^ 1])
        others.append(swap(made, "hid", q))
    x = lax.optimization_barrier((got_hidden, made))[0]
    total = down(my_hid, x, weights, 0, quarter, F32, sums[1])
    x = lax.optimization_barrier((x, total))[0]
    weight_grad = outer(my_dp, my_hid, x, halves)
    for other in others[1:]:
        total = total + other.astype(F32)
    total, got_back, weight_grad = lax.optimization_barrier((total, got_back, weight_grad))
    total, got_back = lax.optimization_barrier((sum_of(total, others[0]), got_back))
    got_out = over_dp(total)

    gate_grad, up_grad, dots = grads(slices, token_key, gate, up, got_back)
    shape = (tokens, TOP, local_ff)
    gate_grad, up_grad = gate_grad.reshape(shape), up_grad.reshape(shape)
    cg = dots.reshape(tokens, TOP) / combine
    bit = 1
    while bit < hid_count:
        cg = cg + swap(cg, "hid", bit)
        bit *= 2
    after = (weight_grad, gate_grad, up_grad, cg)
    mixed = mixed_of(slices, slot_key, weight, got_out, after)
    return jnp.swapaxes(mixed, 0, 1), cg, gate_grad, up_grad, weight_grad


def solution(mesh):
    return jax.shard_map(
        per_device,
        mesh=mesh,
        in_specs=(
            P("dp", None, "hid"),
            P("dp", None, "hid"),
            P("dp", None),
            P("dp", None),
            P("dp", None),
            P("dp", "hid", None),
        ),
        out_specs=(
            P("dp", None, "hid"),
            P("dp", None),
            P("dp", None, "hid"),
            P("dp", None, "hid"),
            P("dp", "hid", None),
        ),
        check_vma=False,
    )
```

```python
import functools

import jax
import jax.numpy as jnp
from jax import lax
from jax.experimental import pallas as pl
from jax.experimental.pallas import tpu as pltpu
from jax.sharding import PartitionSpec as P

E = 8
TOP = 2
CAP = 48
F32 = jnp.float32
BF16 = jnp.bfloat16
I32 = jnp.int32
WIDE = pltpu.CompilerParams(vmem_limit_bytes=63 * 1024 * 1024)
PARAMS = pltpu.CompilerParams(vmem_limit_bytes=40 * 1024 * 1024)
ROWS = (((0,), (0,)), ((), ()))
COLUMNS = (((1,), (1,)), ((), ()))
WORK = 1 / 1000


def whole(a):
    return pl.BlockSpec(a.shape, lambda *_: (0,) * len(a.shape))


def cost(flops, *arrays):
    size = sum(a.size * jnp.dtype(a.dtype).itemsize for a in arrays)
    return pl.CostEstimate(
        flops=int(flops * WORK), bytes_accessed=int(size * WORK), transcendentals=0
    )


def swap(x, axis, bit, after=()):
    if len(after):
        x = lax.optimization_barrier((x, tuple(after)))[0]
    count = lax.axis_size(axis)
    return lax.ppermute(x, axis, [(i, i ^ bit) for i in range(count)])


def ones(table):
    return jnp.where(table, 1.0, 0.0).astype(BF16)


def block_table(d, slices, slot_key):
    key = lax.broadcasted_iota(I32, (CAP, slot_key.shape[1]), 0) + d // slices * CAP
    return key == slot_key


def table_of(slices, slot_key):
    count = E * slices
    return jnp.concatenate([block_table(d, slices, slot_key) for d in range(count)], axis=0)


def scale_kernel(slices, dp_ref, hid_ref, ids_ref, weight_ref, *refs):
    grads, o_refs, key_ref = refs[:slices], refs[slices:-1], refs[-1]
    tokens = ids_ref.shape[1]
    slots = tokens * TOP
    ids = jnp.concatenate([ids_ref[s : s + 1] for s in range(TOP)], axis=1)
    weight = jnp.concatenate([weight_ref[s : s + 1] for s in range(TOP)], axis=1)
    is_expert = lax.broadcasted_iota(I32, (E, slots), 0) == ids
    before = lax.broadcasted_iota(I32, (slots, slots), 0) < lax.broadcasted_iota(
        I32, (slots, slots), 1
    )
    earlier = jnp.dot(ones(is_expert), ones(before), preferred_element_type=F32)
    place = jnp.sum(jnp.where(is_expert, earlier, 0.0), axis=0, keepdims=True)
    slot_key = ids * CAP + place.astype(I32)
    for s in range(TOP):
        key_ref[s : s + 1, :] = slot_key[:, s * tokens : (s + 1) * tokens]
    to = [dp_ref[0] ^ k for k in range(E * slices)]
    table = jnp.concatenate([block_table(d, slices, slot_key) for d in to], axis=0)
    row_weight = jnp.sum(jnp.where(table, weight, 0.0), axis=1, keepdims=True)
    picks = ones(table[:, :tokens]) + ones(table[:, tokens:])
    picked = [jnp.dot(picks, g[...], preferred_element_type=F32) for g in grads]
    for k, o_ref in enumerate(o_refs):
        at = slice(k * CAP, (k + 1) * CAP)
        rows = picked[0][at]
        for j in range(1, slices):
            rows = jnp.where(to[k] % slices == j, picked[j][at], rows)
        o_ref[...] = (rows * row_weight[at]).astype(BF16)


def send_scaled(my_dp, my_hid, ids, weight, out_grad, slices, quarter):
    tokens = ids.shape[1]
    hid_count = out_grad.shape[1] // (slices * quarter)
    outs = [jax.ShapeDtypeStruct((CAP, quarter), BF16)] * (E * slices)
    key = jax.ShapeDtypeStruct(ids.shape, I32)

    def part(j):
        return pl.BlockSpec((tokens, quarter), lambda i, d, h: (0, j * hid_count + h[0]))

    return pl.pallas_call(
        functools.partial(scale_kernel, slices),
        grid_spec=pltpu.PrefetchScalarGridSpec(
            num_scalar_prefetch=2,
            grid=(1,),
            in_specs=[whole(ids), whole(weight)] + [part(j) for j in range(slices)],
            out_specs=[whole(o) for o in outs] + [whole(key)],
        ),
        out_shape=outs + [key],
        compiler_params=WIDE,
        cost_estimate=cost(0, *outs),
        name="send_scaled",
    )(my_dp, my_hid, ids, weight, *[out_grad] * slices)


def hidden_of(gate, up):
    sig = 1.0 / (1.0 + jnp.exp(-gate))
    return sig, (gate * sig * up).astype(BF16)


def send_kernel(slices, dp_ref, key_ref, gate_ref, up_ref, *o_refs):
    hidden = hidden_of(gate_ref[...].astype(F32), up_ref[...].astype(F32))[1]
    blocks = [block_table(dp_ref[0] ^ k, slices, key_ref[...]) for k in range(len(o_refs))]
    table = ones(jnp.concatenate(blocks, axis=0))
    rows = jnp.dot(table, hidden, preferred_element_type=F32).astype(BF16)
    for k, o_ref in enumerate(o_refs):
        o_ref[...] = rows[k * CAP : (k + 1) * CAP]


def send_hidden(my_dp, slices, slot_key, gate, up):
    slots, depth = gate.shape
    block = 512
    outs = [jax.ShapeDtypeStruct((CAP, depth), BF16)] * (E * slices)
    part = pl.BlockSpec((slots, block), lambda i, d: (0, i))
    return pl.pallas_call(
        functools.partial(send_kernel, slices),
        grid_spec=pltpu.PrefetchScalarGridSpec(
            num_scalar_prefetch=1,
            grid=(depth // block,),
            in_specs=[whole(slot_key), part, part],
            out_specs=[pl.BlockSpec((CAP, block), lambda i, d: (0, i)) for _ in outs],
        ),
        out_shape=outs,
        compiler_params=PARAMS,
        cost_estimate=cost(0, gate, up, *outs),
        name="send_hidden",
    )(my_dp, slot_key, gate, up)


def down_kernel(added, hid_ref, x_ref, w_ref, *refs):
    out = jnp.dot(x_ref[...], w_ref[...], preferred_element_type=F32)
    for a in refs[:added]:
        out = out + a[...].astype(F32)
    o_ref = refs[added]
    o_ref[...] = out.astype(o_ref.dtype)


def down(my_hid, x, weights, q, quarter, dtype, params, *add):
    rows, depth = x.shape
    block = min(512, quarter)
    per = quarter // block
    out = jax.ShapeDtypeStruct((rows, quarter), dtype)
    return pl.pallas_call(
        functools.partial(down_kernel, len(add)),
        grid_spec=pltpu.PrefetchScalarGridSpec(
            num_scalar_prefetch=1,
            grid=(per,),
            in_specs=[
                whole(x),
                pl.BlockSpec((depth, block), lambda j, h: (0, (h[0] ^ q) * per + j)),
            ]
            + [pl.BlockSpec((rows, block), lambda j, h: (0, j)) for _ in add],
            out_specs=pl.BlockSpec((rows, block), lambda j, h: (0, j)),
        ),
        out_shape=out,
        compiler_params=params,
        cost_estimate=cost(
            2 * rows * depth * quarter, x, out, jax.ShapeDtypeStruct((depth, quarter), BF16)
        ),
        name="down",
    )(my_hid, x, weights, *add)


def first_down_kernel(count, dp_ref, hid_ref, *refs):
    blocks, w_ref, o_ref, x_ref = refs[:count], *refs[count:]

    @pl.when(pl.program_id(0) == 0)
    def _():
        for k, b in enumerate(blocks):
            x_ref[rows_of(dp_ref, k), :] = b[...]

    o_ref[...] = jnp.dot(x_ref[...], w_ref[...], preferred_element_type=F32).astype(BF16)


def first_down(my_dp, my_hid, blocks, weights, q, quarter):
    rows, depth = CAP * len(blocks), blocks[0].shape[1]
    block = min(512, quarter)
    per = quarter // block
    outs = [jax.ShapeDtypeStruct((rows, quarter), BF16), jax.ShapeDtypeStruct((rows, depth), BF16)]
    return pl.pallas_call(
        functools.partial(first_down_kernel, len(blocks)),
        grid_spec=pltpu.PrefetchScalarGridSpec(
            num_scalar_prefetch=2,
            grid=(per,),
            in_specs=[whole(b) for b in blocks]
            + [pl.BlockSpec((depth, block), lambda j, d, h: (0, (h[0] ^ q) * per + j))],
            out_specs=[pl.BlockSpec((rows, block), lambda j, d, h: (0, j)), whole(outs[1])],
        ),
        out_shape=outs,
        compiler_params=PARAMS,
        cost_estimate=cost(
            2 * rows * depth * quarter, *outs, jax.ShapeDtypeStruct((depth, quarter), BF16)
        ),
        name="first_down",
    )(my_dp, my_hid, *blocks, weights)


def sum_kernel(a_ref, b_ref, o_ref):
    o_ref[...] = (a_ref[...] + b_ref[...].astype(F32)).astype(BF16)


def sum_of(a, b):
    rows, width = a.shape
    block = min(512, width)
    part = pl.BlockSpec((rows, block), lambda i: (0, i))
    out = jax.ShapeDtypeStruct((rows, width), BF16)
    return pl.pallas_call(
        sum_kernel,
        grid=(width // block,),
        in_specs=[part, part],
        out_specs=part,
        out_shape=out,
        compiler_params=WIDE,
        cost_estimate=cost(0, a, b, out),
        name="sum_of",
    )(a, b)


def stack_kernel(*refs):
    *blocks, o_ref = refs
    for k, b in enumerate(blocks):
        o_ref[k * CAP : (k + 1) * CAP, :] = b[...]


def stack(blocks):
    out = jax.ShapeDtypeStruct((CAP * len(blocks), blocks[0].shape[1]), BF16)
    return pl.pallas_call(
        stack_kernel,
        grid=(1,),
        in_specs=[whole(b) for b in blocks],
        out_specs=whole(out),
        out_shape=out,
        compiler_params=PARAMS,
        cost_estimate=cost(0, out, out),
        name="stack",
    )(*blocks)


def rows_of(dp_ref, k):
    return pl.ds(pl.multiple_of((dp_ref[0] ^ k) * CAP, CAP), CAP)


def in_order(dp_ref, halves, y_ref):
    per = halves[0].shape[0] // CAP
    for n, half in enumerate(halves):
        for k in range(per):
            y_ref[n // 2, rows_of(dp_ref, n % 2 * per + k), :] = half[k * CAP : (k + 1) * CAP, :]


def quarter_at(hid_ref, q, quarter):
    return pl.ds(pl.multiple_of((hid_ref[0] ^ q) * quarter, 128), quarter)


def back_kernel(dp_ref, hid_ref, *refs):
    *halves, w_ref, o_ref, y_ref = refs

    @pl.when(pl.program_id(0) == 0)
    def _():
        in_order(dp_ref, halves, y_ref)

    count, _, quarter = y_ref.shape
    total = None
    for q in range(count):
        w = w_ref[:, quarter_at(hid_ref, q, quarter)]
        term = lax.dot_general(y_ref[q], w, COLUMNS, preferred_element_type=F32)
        total = term if total is None else total + term
    o_ref[...] = total.astype(BF16)


def back(my_dp, my_hid, halves, weights):
    rows, quarter = 2 * halves[0].shape[0], halves[0].shape[1]
    depth, width = weights.shape
    block = 256
    out = jax.ShapeDtypeStruct((rows, depth), BF16)
    y = jax.ShapeDtypeStruct((width // quarter, rows, quarter), BF16)
    return pl.pallas_call(
        back_kernel,
        grid_spec=pltpu.PrefetchScalarGridSpec(
            num_scalar_prefetch=2,
            grid=(depth // block,),
            in_specs=[whole(p) for p in halves]
            + [pl.BlockSpec((block, width), lambda i, d, h: (i, 0))],
            out_specs=[pl.BlockSpec((rows, block), lambda i, d, h: (0, i)), whole(y)],
        ),
        out_shape=[out, y],
        compiler_params=PARAMS,
        cost_estimate=cost(2 * rows * depth * width, *halves, weights, out),
        name="back",
    )(my_dp, my_hid, *halves, weights)


def outer_kernel(hid_ref, x_ref, y_ref, o_ref):
    count, _, quarter = y_ref.shape
    x = x_ref[...]
    for q in range(count):
        o_ref[0, :, quarter_at(hid_ref, q, quarter)] = lax.dot_general(
            x, y_ref[q], ROWS, preferred_element_type=F32
        ).astype(BF16)


def outer(my_hid, x, y):
    rows, depth = x.shape
    width = y.shape[0] * y.shape[2]
    block = 256
    out = jax.ShapeDtypeStruct((1, depth, width), BF16)
    return pl.pallas_call(
        outer_kernel,
        grid_spec=pltpu.PrefetchScalarGridSpec(
            num_scalar_prefetch=1,
            grid=(depth // block,),
            in_specs=[pl.BlockSpec((rows, block), lambda i, h: (0, i)), whole(y)],
            out_specs=pl.BlockSpec((1, block, width), lambda i, h: (0, i, 0)),
        ),
        out_shape=out,
        compiler_params=WIDE,
        cost_estimate=cost(2 * rows * depth * width, x, y, out),
        name="outer",
    )(my_hid, x, y)


def grads_kernel(slices, key_ref, gate_ref, up_ref, back_ref, dgate_ref, dup_ref, dot_ref):
    table = ones(table_of(slices, key_ref[...]))
    h = lax.dot_general(table, back_ref[...], ROWS, preferred_element_type=F32)
    g, u = gate_ref[...].astype(F32), up_ref[...].astype(F32)
    sig, hidden = hidden_of(g, u)
    dgate_ref[...] = (h * u * sig * (1.0 + g * (1.0 - sig))).astype(BF16)
    dup_ref[...] = (h * g * sig).astype(BF16)
    dots = jnp.sum(hidden.astype(F32) * h, axis=1, keepdims=True)

    @pl.when(pl.program_id(0) == 0)
    def _():
        dot_ref[...] = dots

    @pl.when(pl.program_id(0) > 0)
    def _():
        dot_ref[...] += dots


def grads(slices, slot_key, gate, up, got_back):
    slots, depth = gate.shape
    rows = got_back.shape[0]
    block = 512
    part = pl.BlockSpec((slots, block), lambda i: (0, i))
    out = jax.ShapeDtypeStruct(gate.shape, BF16)
    dots = jax.ShapeDtypeStruct((slots, 1), F32)
    return pl.pallas_call(
        functools.partial(grads_kernel, slices),
        grid=(depth // block,),
        in_specs=[
            whole(slot_key),
            part,
            part,
            pl.BlockSpec((rows, block), lambda i: (0, i)),
        ],
        out_specs=[part, part, whole(dots)],
        out_shape=[out, out, dots],
        compiler_params=WIDE,
        cost_estimate=cost(0, gate, up, got_back, out, out),
        name="grads",
    )(slot_key, gate, up, got_back)


def mix_kernel(slices, key_ref, weight_ref, x_ref, *refs):
    o_ref = refs[-1]
    tokens = key_ref.shape[1]
    x = x_ref[...]
    for j in range(slices):
        rows = []
        for d in range(E * slices):
            row = jnp.zeros((CAP, tokens), F32)
            if d % slices == j:
                for s in range(TOP):
                    hit = block_table(d, slices, key_ref[s : s + 1, :])
                    row = jnp.where(hit, weight_ref[s : s + 1, :], row)
            rows.append(row)
        left = jnp.concatenate(rows, axis=0)
        total = None
        for _ in range(3):
            part = left.astype(BF16)
            left = left - part.astype(F32)
            term = lax.dot_general(part, x, ROWS, preferred_element_type=F32)
            total = term if total is None else total + term
        o_ref[j] = total.astype(BF16)


def mixed_of(slices, slot_key, weight, got_out, after):
    tokens = slot_key.shape[1]
    rows, quarter = got_out.shape
    out = jax.ShapeDtypeStruct((slices, tokens, quarter), BF16)
    return pl.pallas_call(
        functools.partial(mix_kernel, slices),
        grid=(1,),
        in_specs=[whole(slot_key), whole(weight), whole(got_out)]
        + [pl.BlockSpec(memory_space=pl.ANY) for _ in after],
        out_specs=whole(out),
        out_shape=out,
        compiler_params=PARAMS,
        cost_estimate=cost(0, got_out, out),
        name="mixed",
    )(slot_key, weight, got_out, *after)


def per_device(gate_pre, up_pre, out_grad, combine, expert_ids, down_weight):
    dp_count = lax.axis_size("dp")
    hid_count = lax.axis_size("hid")
    my_dp = lax.axis_index("dp").astype(I32).reshape(1)
    my_hid = lax.axis_index("hid").astype(I32).reshape(1)
    slices = dp_count // E
    tokens = gate_pre.shape[0]
    local_ff = gate_pre.shape[2]
    quarter = down_weight.shape[2] // hid_count
    slots = tokens * TOP
    weights = down_weight[0]
    ids, weight = expert_ids.T, combine.T

    def over_dp(x):
        return lax.all_to_all(x, "dp", split_axis=0, concat_axis=0, tiled=True)

    *scaled, slot_key = send_scaled(my_dp, my_hid, ids, weight, out_grad, slices, quarter)
    gate, up = gate_pre.reshape(slots, local_ff), up_pre.reshape(slots, local_ff)
    token_key = slot_key.T.reshape(1, slots)
    hidden = send_hidden(my_dp, slices, token_key, gate, up)

    near, far = list(range(dp_count // 2 - 1, 0, -1)), list(range(dp_count - 1, dp_count // 2 - 1, -1))
    got = {0: scaled[0]}
    for k in far[:2] + near:
        got[k] = swap(scaled[k], "dp", k)
    for k, ahead in zip(far[2:], near * len(far)):
        got[k] = swap(scaled[k], "dp", k, [got[ahead]])
    own = [stack([got[k] for k in part]) for part in ([0, *near[::-1]], far[::-1])]
    own[0] = lax.optimization_barrier((own[0], hidden))[0]
    got_hidden = {0: hidden[0]}
    for k, ahead in zip(far[:3], far[2:4] + far[3:4]):
        got_hidden[k] = swap(hidden[k], "dp", k, [got[ahead]])
    halves = [{0: x} for x in own]
    bit = hid_count // 2
    for piece in halves:
        piece[bit] = swap(piece[0], "hid", bit)
    while bit > 1:
        bit //= 2
        for piece in halves:
            for q in sorted(piece):
                if q ^ bit not in piece:
                    ahead = [got_hidden[k] for k in far[:2]] if q and piece is halves[1] else []
                    piece[q ^ bit] = swap(piece[q], "hid", bit, ahead)
    got_hidden[near[0]] = swap(hidden[near[0]], "dp", near[0], [halves[1][1]])
    for i, k in enumerate(far[3:] + near[1:]):
        got_hidden[k] = swap(hidden[k], "dp", k, [got_hidden[far[min(i, 1)]]])
    halves = [piece[q] for q in range(hid_count) for piece in halves]
    sent_back, y = back(my_dp, my_hid, halves, weights)
    got_hidden = [got_hidden[k] for k in range(dp_count)]
    got_hidden, sent_back = lax.optimization_barrier((got_hidden, sent_back))

    sums, others = {}, []
    for q in range(hid_count - 1, 0, -2):
        if q == hid_count - 1:
            made, x = first_down(my_dp, my_hid, got_hidden, weights, q, quarter)
        else:
            made = down(my_hid, x, weights, q, quarter, BF16, PARAMS)
        sums[q] = swap(made, "hid", 1)
        if q == hid_count - 1:
            sent_back = lax.optimization_barrier((sent_back, made))[0]
            got_back = over_dp(sent_back)
        if q > 1:
            made = down(my_hid, x, weights, q - 1, quarter, BF16, PARAMS, sums[q])
            others.append(swap(made, "hid", q - 1))
            x = lax.optimization_barrier((x, made))[0]
    total = down(my_hid, x, weights, 0, quarter, F32, WIDE, sums[1])
    x = lax.optimization_barrier((x, total))[0]
    weight_grad = outer(my_hid, x, y)
    for other in others[1:]:
        total = total + other.astype(F32)
    total, got_back, weight_grad = lax.optimization_barrier((total, got_back, weight_grad))
    total, got_back = lax.optimization_barrier((sum_of(total, others[0]), got_back))
    got_out = over_dp(total)

    gate_grad, up_grad, dots = grads(slices, token_key, gate, up, got_back)
    shape = (tokens, TOP, local_ff)
    gate_grad, up_grad = gate_grad.reshape(shape), up_grad.reshape(shape)
    cg = dots.reshape(tokens, TOP) / combine
    bit = 1
    while bit < hid_count:
        cg = cg + swap(cg, "hid", bit)
        bit *= 2
    after = (weight_grad, gate_grad, up_grad, cg)
    mixed = mixed_of(slices, slot_key, weight, got_out, after)
    return jnp.swapaxes(mixed, 0, 1), cg, gate_grad, up_grad, weight_grad


def solution(mesh):
    return jax.shard_map(
        per_device,
        mesh=mesh,
        in_specs=(
            P("dp", None, "hid"),
            P("dp", None, "hid"),
            P("dp", None),
            P("dp", None),
            P("dp", None),
            P("dp", "hid", None),
        ),
        out_specs=(
            P("dp", None, "hid"),
            P("dp", None),
            P("dp", None, "hid"),
            P("dp", None, "hid"),
            P("dp", "hid", None),
        ),
        check_vma=False,
    )
```

```python
import functools

import jax
import jax.numpy as jnp
from jax import lax
from jax.experimental import pallas as pl
from jax.experimental.pallas import tpu as pltpu
from jax.sharding import PartitionSpec as P

E = 8
TOP = 2
CAP = 48
F32 = jnp.float32
BF16 = jnp.bfloat16
I32 = jnp.int32
WIDE = pltpu.CompilerParams(vmem_limit_bytes=63 * 1024 * 1024)
PARAMS = pltpu.CompilerParams(vmem_limit_bytes=40 * 1024 * 1024)
ROWS = (((0,), (0,)), ((), ()))
COLUMNS = (((1,), (1,)), ((), ()))
WORK = 1 / 1000


def whole(a):
    return pl.BlockSpec(a.shape, lambda *_: (0,) * len(a.shape))


def cost(flops, *arrays):
    size = sum(a.size * jnp.dtype(a.dtype).itemsize for a in arrays)
    return pl.CostEstimate(
        flops=int(flops * WORK), bytes_accessed=int(size * WORK), transcendentals=0
    )


def swap(x, axis, bit, after=()):
    if len(after):
        x = lax.optimization_barrier((x, tuple(after)))[0]
    count = lax.axis_size(axis)
    return lax.ppermute(x, axis, [(i, i ^ bit) for i in range(count)])


def ones(table):
    return jnp.where(table, 1.0, 0.0).astype(BF16)


def block_table(d, slices, slot_key):
    key = lax.broadcasted_iota(I32, (CAP, slot_key.shape[1]), 0) + d // slices * CAP
    return key == slot_key


def table_of(slices, slot_key):
    count = E * slices
    return jnp.concatenate([block_table(d, slices, slot_key) for d in range(count)], axis=0)


def scale_kernel(slices, dp_ref, hid_ref, ids_ref, weight_ref, *refs):
    grads, o_refs, key_ref = refs[:slices], refs[slices:-1], refs[-1]
    tokens = ids_ref.shape[1]
    slots = tokens * TOP
    ids = jnp.concatenate([ids_ref[s : s + 1] for s in range(TOP)], axis=1)
    weight = jnp.concatenate([weight_ref[s : s + 1] for s in range(TOP)], axis=1)
    is_expert = lax.broadcasted_iota(I32, (E, slots), 0) == ids
    before = lax.broadcasted_iota(I32, (slots, slots), 0) < lax.broadcasted_iota(
        I32, (slots, slots), 1
    )
    earlier = jnp.dot(ones(is_expert), ones(before), preferred_element_type=F32)
    place = jnp.sum(jnp.where(is_expert, earlier, 0.0), axis=0, keepdims=True)
    slot_key = ids * CAP + place.astype(I32)
    for s in range(TOP):
        key_ref[s : s + 1, :] = slot_key[:, s * tokens : (s + 1) * tokens]
    to = [dp_ref[0] ^ k for k in range(E * slices)]
    table = jnp.concatenate([block_table(d, slices, slot_key) for d in to], axis=0)
    row_weight = jnp.sum(jnp.where(table, weight, 0.0), axis=1, keepdims=True)
    picks = ones(table[:, :tokens]) + ones(table[:, tokens:])
    picked = [jnp.dot(picks, g[...], preferred_element_type=F32) for g in grads]
    for k, o_ref in enumerate(o_refs):
        at = slice(k * CAP, (k + 1) * CAP)
        rows = picked[0][at]
        for j in range(1, slices):
            rows = jnp.where(to[k] % slices == j, picked[j][at], rows)
        o_ref[...] = (rows * row_weight[at]).astype(BF16)


def send_scaled(my_dp, my_hid, ids, weight, out_grad, slices, quarter):
    tokens = ids.shape[1]
    hid_count = out_grad.shape[1] // (slices * quarter)
    outs = [jax.ShapeDtypeStruct((CAP, quarter), BF16)] * (E * slices)
    key = jax.ShapeDtypeStruct(ids.shape, I32)

    def part(j):
        return pl.BlockSpec((tokens, quarter), lambda i, d, h: (0, j * hid_count + h[0]))

    return pl.pallas_call(
        functools.partial(scale_kernel, slices),
        grid_spec=pltpu.PrefetchScalarGridSpec(
            num_scalar_prefetch=2,
            grid=(1,),
            in_specs=[whole(ids), whole(weight)] + [part(j) for j in range(slices)],
            out_specs=[whole(o) for o in outs] + [whole(key)],
        ),
        out_shape=outs + [key],
        compiler_params=WIDE,
        cost_estimate=cost(0, *outs),
        name="send_scaled",
    )(my_dp, my_hid, ids, weight, *[out_grad] * slices)


def hidden_of(gate, up):
    sig = 1.0 / (1.0 + jnp.exp(-gate))
    return sig, (gate * sig * up).astype(BF16)


def send_kernel(slices, dp_ref, key_ref, gate_ref, up_ref, *o_refs):
    hidden = hidden_of(gate_ref[...].astype(F32), up_ref[...].astype(F32))[1]
    blocks = [block_table(dp_ref[0] ^ k, slices, key_ref[...]) for k in range(len(o_refs))]
    table = ones(jnp.concatenate(blocks, axis=0))
    rows = jnp.dot(table, hidden, preferred_element_type=F32).astype(BF16)
    for k, o_ref in enumerate(o_refs):
        o_ref[...] = rows[k * CAP : (k + 1) * CAP]


def send_hidden(my_dp, slices, slot_key, gate, up):
    slots, depth = gate.shape
    block = 512
    outs = [jax.ShapeDtypeStruct((CAP, depth), BF16)] * (E * slices)
    part = pl.BlockSpec((slots, block), lambda i, d: (0, i))
    return pl.pallas_call(
        functools.partial(send_kernel, slices),
        grid_spec=pltpu.PrefetchScalarGridSpec(
            num_scalar_prefetch=1,
            grid=(depth // block,),
            in_specs=[whole(slot_key), part, part],
            out_specs=[pl.BlockSpec((CAP, block), lambda i, d: (0, i)) for _ in outs],
        ),
        out_shape=outs,
        compiler_params=PARAMS,
        cost_estimate=cost(0, gate, up, *outs),
        name="send_hidden",
    )(my_dp, slot_key, gate, up)


def down_kernel(added, hid_ref, x_ref, w_ref, *refs):
    out = jnp.dot(x_ref[...], w_ref[...], preferred_element_type=F32)
    for a in refs[:added]:
        out = out + a[...].astype(F32)
    o_ref = refs[added]
    o_ref[...] = out.astype(o_ref.dtype)


def down(my_hid, x, weights, q, quarter, dtype, params, *add):
    rows, depth = x.shape
    block = min(512, quarter)
    per = quarter // block
    out = jax.ShapeDtypeStruct((rows, quarter), dtype)
    return pl.pallas_call(
        functools.partial(down_kernel, len(add)),
        grid_spec=pltpu.PrefetchScalarGridSpec(
            num_scalar_prefetch=1,
            grid=(per,),
            in_specs=[
                whole(x),
                pl.BlockSpec((depth, block), lambda j, h: (0, (h[0] ^ q) * per + j)),
            ]
            + [pl.BlockSpec((rows, block), lambda j, h: (0, j)) for _ in add],
            out_specs=pl.BlockSpec((rows, block), lambda j, h: (0, j)),
        ),
        out_shape=out,
        compiler_params=params,
        cost_estimate=cost(
            2 * rows * depth * quarter, x, out, jax.ShapeDtypeStruct((depth, quarter), BF16)
        ),
        name="down",
    )(my_hid, x, weights, *add)


def first_down_kernel(count, dp_ref, hid_ref, *refs):
    blocks, w_ref, o_ref, x_ref = refs[:count], *refs[count:]

    @pl.when(pl.program_id(0) == 0)
    def _():
        for k, b in enumerate(blocks):
            x_ref[rows_of(dp_ref, k), :] = b[...]

    o_ref[...] = jnp.dot(x_ref[...], w_ref[...], preferred_element_type=F32).astype(BF16)


def first_down(my_dp, my_hid, blocks, weights, q, quarter):
    rows, depth = CAP * len(blocks), blocks[0].shape[1]
    block = min(512, quarter)
    per = quarter // block
    outs = [jax.ShapeDtypeStruct((rows, quarter), BF16), jax.ShapeDtypeStruct((rows, depth), BF16)]
    return pl.pallas_call(
        functools.partial(first_down_kernel, len(blocks)),
        grid_spec=pltpu.PrefetchScalarGridSpec(
            num_scalar_prefetch=2,
            grid=(per,),
            in_specs=[whole(b) for b in blocks]
            + [pl.BlockSpec((depth, block), lambda j, d, h: (0, (h[0] ^ q) * per + j))],
            out_specs=[pl.BlockSpec((rows, block), lambda j, d, h: (0, j)), whole(outs[1])],
        ),
        out_shape=outs,
        compiler_params=PARAMS,
        cost_estimate=cost(
            2 * rows * depth * quarter, *outs, jax.ShapeDtypeStruct((depth, quarter), BF16)
        ),
        name="first_down",
    )(my_dp, my_hid, *blocks, weights)


def sum_kernel(a_ref, b_ref, o_ref):
    o_ref[...] = (a_ref[...] + b_ref[...].astype(F32)).astype(BF16)


def sum_of(a, b):
    rows, width = a.shape
    block = 2 * CAP
    part = pl.BlockSpec((block, width), lambda i: (i, 0))
    out = jax.ShapeDtypeStruct((rows, width), BF16)
    return pl.pallas_call(
        sum_kernel,
        grid=(rows // block,),
        in_specs=[part, part],
        out_specs=part,
        out_shape=out,
        compiler_params=WIDE,
        cost_estimate=cost(0, a, b, out),
        name="sum_of",
    )(a, b)


def stack_kernel(*refs):
    *blocks, o_ref = refs
    for k, b in enumerate(blocks):
        o_ref[k * CAP : (k + 1) * CAP, :] = b[...]


def stack(blocks):
    out = jax.ShapeDtypeStruct((CAP * len(blocks), blocks[0].shape[1]), BF16)
    return pl.pallas_call(
        stack_kernel,
        grid=(1,),
        in_specs=[whole(b) for b in blocks],
        out_specs=whole(out),
        out_shape=out,
        compiler_params=PARAMS,
        cost_estimate=cost(0, out, out),
        name="stack",
    )(*blocks)


def rows_of(dp_ref, k):
    return pl.ds(pl.multiple_of((dp_ref[0] ^ k) * CAP, CAP), CAP)


def in_order(dp_ref, halves, y_ref):
    per = halves[0].shape[0] // CAP
    for n, half in enumerate(halves):
        for k in range(per):
            y_ref[n // 2, rows_of(dp_ref, n % 2 * per + k), :] = half[k * CAP : (k + 1) * CAP, :]


def quarter_at(hid_ref, q, quarter):
    return pl.ds(pl.multiple_of((hid_ref[0] ^ q) * quarter, 128), quarter)


def back_kernel(dp_ref, hid_ref, *refs):
    *halves, w_ref, o_ref, y_ref = refs

    @pl.when(pl.program_id(0) == 0)
    def _():
        in_order(dp_ref, halves, y_ref)

    count, _, quarter = y_ref.shape
    total = None
    for q in range(count):
        w = w_ref[:, quarter_at(hid_ref, q, quarter)]
        term = lax.dot_general(y_ref[q], w, COLUMNS, preferred_element_type=F32)
        total = term if total is None else total + term
    o_ref[...] = total.astype(BF16)


def back(my_dp, my_hid, halves, weights):
    rows, quarter = 2 * halves[0].shape[0], halves[0].shape[1]
    depth, width = weights.shape
    block = 256
    out = jax.ShapeDtypeStruct((rows, depth), BF16)
    y = jax.ShapeDtypeStruct((width // quarter, rows, quarter), BF16)
    return pl.pallas_call(
        back_kernel,
        grid_spec=pltpu.PrefetchScalarGridSpec(
            num_scalar_prefetch=2,
            grid=(depth // block,),
            in_specs=[whole(p) for p in halves]
            + [pl.BlockSpec((block, width), lambda i, d, h: (i, 0))],
            out_specs=[pl.BlockSpec((rows, block), lambda i, d, h: (0, i)), whole(y)],
        ),
        out_shape=[out, y],
        compiler_params=PARAMS,
        cost_estimate=cost(2 * rows * depth * width, *halves, weights, out),
        name="back",
    )(my_dp, my_hid, *halves, weights)


def outer_kernel(hid_ref, x_ref, y_ref, o_ref):
    count, _, quarter = y_ref.shape
    x = x_ref[...]
    for q in range(count):
        o_ref[0, :, quarter_at(hid_ref, q, quarter)] = lax.dot_general(
            x, y_ref[q], ROWS, preferred_element_type=F32
        ).astype(BF16)


def outer(my_hid, x, y):
    rows, depth = x.shape
    width = y.shape[0] * y.shape[2]
    block = 256
    out = jax.ShapeDtypeStruct((1, depth, width), BF16)
    return pl.pallas_call(
        outer_kernel,
        grid_spec=pltpu.PrefetchScalarGridSpec(
            num_scalar_prefetch=1,
            grid=(depth // block,),
            in_specs=[pl.BlockSpec((rows, block), lambda i, h: (0, i)), whole(y)],
            out_specs=pl.BlockSpec((1, block, width), lambda i, h: (0, i, 0)),
        ),
        out_shape=out,
        compiler_params=WIDE,
        cost_estimate=cost(2 * rows * depth * width, x, y, out),
        name="outer",
    )(my_hid, x, y)


def grads_kernel(slices, key_ref, gate_ref, up_ref, back_ref, dgate_ref, dup_ref, dot_ref):
    table = ones(table_of(slices, key_ref[...]))
    h = lax.dot_general(table, back_ref[...], ROWS, preferred_element_type=F32)
    g, u = gate_ref[...].astype(F32), up_ref[...].astype(F32)
    sig, hidden = hidden_of(g, u)
    dgate_ref[...] = (h * u * sig * (1.0 + g * (1.0 - sig))).astype(BF16)
    dup_ref[...] = (h * g * sig).astype(BF16)
    dots = jnp.sum(hidden.astype(F32) * h, axis=1, keepdims=True)

    @pl.when(pl.program_id(0) == 0)
    def _():
        dot_ref[...] = dots

    @pl.when(pl.program_id(0) > 0)
    def _():
        dot_ref[...] += dots


def grads(slices, slot_key, gate, up, got_back):
    slots, depth = gate.shape
    rows = got_back.shape[0]
    block = 512
    part = pl.BlockSpec((slots, block), lambda i: (0, i))
    out = jax.ShapeDtypeStruct(gate.shape, BF16)
    dots = jax.ShapeDtypeStruct((slots, 1), F32)
    return pl.pallas_call(
        functools.partial(grads_kernel, slices),
        grid=(depth // block,),
        in_specs=[
            whole(slot_key),
            part,
            part,
            pl.BlockSpec((rows, block), lambda i: (0, i)),
        ],
        out_specs=[part, part, whole(dots)],
        out_shape=[out, out, dots],
        compiler_params=WIDE,
        cost_estimate=cost(0, gate, up, got_back, out, out),
        name="grads",
    )(slot_key, gate, up, got_back)


def mix_kernel(slices, key_ref, weight_ref, x_ref, *refs):
    o_ref = refs[-1]
    tokens = key_ref.shape[1]
    x = x_ref[...]
    for j in range(slices):
        rows = []
        for d in range(E * slices):
            row = jnp.zeros((CAP, tokens), F32)
            if d % slices == j:
                for s in range(TOP):
                    hit = block_table(d, slices, key_ref[s : s + 1, :])
                    row = jnp.where(hit, weight_ref[s : s + 1, :], row)
            rows.append(row)
        left = jnp.concatenate(rows, axis=0)
        total = None
        for _ in range(3):
            part = left.astype(BF16)
            left = left - part.astype(F32)
            term = lax.dot_general(part, x, ROWS, preferred_element_type=F32)
            total = term if total is None else total + term
        o_ref[j] = total.astype(BF16)


def mixed_of(slices, slot_key, weight, got_out, after):
    tokens = slot_key.shape[1]
    rows, quarter = got_out.shape
    out = jax.ShapeDtypeStruct((slices, tokens, quarter), BF16)
    return pl.pallas_call(
        functools.partial(mix_kernel, slices),
        grid=(1,),
        in_specs=[whole(slot_key), whole(weight), whole(got_out)]
        + [pl.BlockSpec(memory_space=pl.ANY) for _ in after],
        out_specs=whole(out),
        out_shape=out,
        compiler_params=PARAMS,
        cost_estimate=cost(0, got_out, out),
        name="mixed",
    )(slot_key, weight, got_out, *after)


def per_device(gate_pre, up_pre, out_grad, combine, expert_ids, down_weight):
    dp_count = lax.axis_size("dp")
    hid_count = lax.axis_size("hid")
    my_dp = lax.axis_index("dp").astype(I32).reshape(1)
    my_hid = lax.axis_index("hid").astype(I32).reshape(1)
    slices = dp_count // E
    tokens = gate_pre.shape[0]
    local_ff = gate_pre.shape[2]
    quarter = down_weight.shape[2] // hid_count
    slots = tokens * TOP
    weights = down_weight[0]
    ids, weight = expert_ids.T, combine.T

    def over_dp(x):
        return lax.all_to_all(x, "dp", split_axis=0, concat_axis=0, tiled=True)

    *scaled, slot_key = send_scaled(my_dp, my_hid, ids, weight, out_grad, slices, quarter)
    gate, up = gate_pre.reshape(slots, local_ff), up_pre.reshape(slots, local_ff)
    token_key = slot_key.T.reshape(1, slots)
    hidden = send_hidden(my_dp, slices, token_key, gate, up)

    near, far = list(range(dp_count // 2 - 1, 0, -1)), list(range(dp_count - 1, dp_count // 2 - 1, -1))
    got = {0: scaled[0]}
    for k in far[:2] + near:
        got[k] = swap(scaled[k], "dp", k)
    for k, ahead in zip(far[2:], near * len(far)):
        got[k] = swap(scaled[k], "dp", k, [got[ahead]])
    own = [stack([got[k] for k in part]) for part in ([0, *near[::-1]], far[::-1])]
    own[0] = lax.optimization_barrier((own[0], hidden))[0]
    halves = [{0: x} for x in own]
    bit = hid_count // 2
    for piece in halves:
        piece[bit] = swap(piece[0], "hid", bit)
    got_hidden = {0: hidden[0]}
    for k, ahead in zip(far[:3], (got[far[2]], got[far[3]], got[far[3]])):
        got_hidden[k] = swap(hidden[k], "dp", k, [ahead])
    while bit > 1:
        bit //= 2
        for piece in halves:
            for q in sorted(piece):
                if q ^ bit not in piece:
                    ahead = [got_hidden[k] for k in far[:2]] if q and piece is halves[1] else []
                    piece[q ^ bit] = swap(piece[q], "hid", bit, ahead)
    got_hidden[near[0]] = swap(hidden[near[0]], "dp", near[0], [halves[1][1]])
    for i, k in enumerate(far[3:] + near[1:]):
        got_hidden[k] = swap(hidden[k], "dp", k, [got_hidden[far[min(i, 1)]]])
    halves = [piece[q] for q in range(hid_count) for piece in halves]
    sent_back, y = back(my_dp, my_hid, halves, weights)
    got_hidden = [got_hidden[k] for k in range(dp_count)]
    got_hidden, sent_back = lax.optimization_barrier((got_hidden, sent_back))

    got_back = over_dp(sent_back)
    sums, others = {}, []
    for q in range(hid_count - 1, 0, -2):
        if not sums:
            made, x = first_down(my_dp, my_hid, got_hidden, weights, q, quarter)
        else:
            made = down(my_hid, x, weights, q, quarter, BF16, PARAMS)
        sums[q] = swap(made, "hid", 1)
    x = lax.optimization_barrier((x, made))[0]
    for q in range(hid_count - 2, 0, -2):
        made = down(my_hid, x, weights, q, quarter, BF16, PARAMS, sums[q + 1])
        others.append(swap(made, "hid", q))
    x = lax.optimization_barrier((x, made))[0]
    total = down(my_hid, x, weights, 0, quarter, F32, WIDE, sums[1])
    x = lax.optimization_barrier((x, total))[0]
    weight_grad = outer(my_hid, x, y)
    for other in others[1:]:
        total = total + other.astype(F32)
    total, got_back, weight_grad = lax.optimization_barrier((total, got_back, weight_grad))
    total, got_back = lax.optimization_barrier((sum_of(total, others[0]), got_back))
    got_out = over_dp(total)

    gate_grad, up_grad, dots = grads(slices, token_key, gate, up, got_back)
    shape = (tokens, TOP, local_ff)
    gate_grad, up_grad = gate_grad.reshape(shape), up_grad.reshape(shape)
    cg = dots.reshape(tokens, TOP) / combine
    bit = 1
    while bit < hid_count:
        cg = cg + swap(cg, "hid", bit)
        bit *= 2
    after = (weight_grad, gate_grad, up_grad, cg)
    mixed = mixed_of(slices, slot_key, weight, got_out, after)
    return jnp.swapaxes(mixed, 0, 1), cg, gate_grad, up_grad, weight_grad


def solution(mesh):
    return jax.shard_map(
        per_device,
        mesh=mesh,
        in_specs=(
            P("dp", None, "hid"),
            P("dp", None, "hid"),
            P("dp", None),
            P("dp", None),
            P("dp", None),
            P("dp", "hid", None),
        ),
        out_specs=(
            P("dp", None, "hid"),
            P("dp", None),
            P("dp", None, "hid"),
            P("dp", None, "hid"),
            P("dp", "hid", None),
        ),
        check_vma=False,
    )
```

```python
import functools

import jax
import jax.numpy as jnp
from jax import lax
from jax.experimental import pallas as pl
from jax.experimental.pallas import tpu as pltpu
from jax.sharding import PartitionSpec as P

E = 8
TOP = 2
CAP = 48
F32 = jnp.float32
BF16 = jnp.bfloat16
I32 = jnp.int32
WIDE = pltpu.CompilerParams(vmem_limit_bytes=63 * 1024 * 1024)
PARAMS = pltpu.CompilerParams(vmem_limit_bytes=40 * 1024 * 1024)
ROWS = (((0,), (0,)), ((), ()))
COLUMNS = (((1,), (1,)), ((), ()))
WORK = 1 / 1000


def whole(a):
    return pl.BlockSpec(a.shape, lambda *_: (0,) * len(a.shape))


def cost(flops, *arrays):
    size = sum(a.size * jnp.dtype(a.dtype).itemsize for a in arrays)
    return pl.CostEstimate(
        flops=int(flops * WORK), bytes_accessed=int(size * WORK), transcendentals=0
    )


def swap(x, axis, bit, after=()):
    if len(after):
        x = lax.optimization_barrier((x, tuple(after)))[0]
    count = lax.axis_size(axis)
    return lax.ppermute(x, axis, [(i, i ^ bit) for i in range(count)])


def ones(table):
    return jnp.where(table, 1.0, 0.0).astype(BF16)


def block_table(d, slices, slot_key):
    key = lax.broadcasted_iota(I32, (CAP, slot_key.shape[1]), 0) + d // slices * CAP
    return key == slot_key


def table_of(slices, slot_key):
    count = E * slices
    return jnp.concatenate([block_table(d, slices, slot_key) for d in range(count)], axis=0)


def scale_kernel(slices, dp_ref, hid_ref, ids_ref, weight_ref, *refs):
    grads, o_refs, key_ref = refs[:slices], refs[slices:-1], refs[-1]
    tokens = ids_ref.shape[1]
    slots = tokens * TOP
    ids = jnp.concatenate([ids_ref[s : s + 1] for s in range(TOP)], axis=1)
    weight = jnp.concatenate([weight_ref[s : s + 1] for s in range(TOP)], axis=1)
    is_expert = lax.broadcasted_iota(I32, (E, slots), 0) == ids
    before = lax.broadcasted_iota(I32, (slots, slots), 0) < lax.broadcasted_iota(
        I32, (slots, slots), 1
    )
    earlier = jnp.dot(ones(is_expert), ones(before), preferred_element_type=F32)
    place = jnp.sum(jnp.where(is_expert, earlier, 0.0), axis=0, keepdims=True)
    slot_key = ids * CAP + place.astype(I32)
    for s in range(TOP):
        key_ref[s : s + 1, :] = slot_key[:, s * tokens : (s + 1) * tokens]
    to = [dp_ref[0] ^ k for k in range(E * slices)]
    table = jnp.concatenate([block_table(d, slices, slot_key) for d in to], axis=0)
    row_weight = jnp.sum(jnp.where(table, weight, 0.0), axis=1, keepdims=True)
    picks = ones(table[:, :tokens]) + ones(table[:, tokens:])
    picked = [jnp.dot(picks, g[...], preferred_element_type=F32) for g in grads]
    for k, o_ref in enumerate(o_refs):
        at = slice(k * CAP, (k + 1) * CAP)
        rows = picked[0][at]
        for j in range(1, slices):
            rows = jnp.where(to[k] % slices == j, picked[j][at], rows)
        o_ref[...] = (rows * row_weight[at]).astype(BF16)


def send_scaled(my_dp, my_hid, ids, weight, out_grad, slices, quarter):
    tokens = ids.shape[1]
    hid_count = out_grad.shape[1] // (slices * quarter)
    outs = [jax.ShapeDtypeStruct((CAP, quarter), BF16)] * (E * slices)
    key = jax.ShapeDtypeStruct(ids.shape, I32)

    def part(j):
        return pl.BlockSpec((tokens, quarter), lambda i, d, h: (0, j * hid_count + h[0]))

    return pl.pallas_call(
        functools.partial(scale_kernel, slices),
        grid_spec=pltpu.PrefetchScalarGridSpec(
            num_scalar_prefetch=2,
            grid=(1,),
            in_specs=[whole(ids), whole(weight)] + [part(j) for j in range(slices)],
            out_specs=[whole(o) for o in outs] + [whole(key)],
        ),
        out_shape=outs + [key],
        compiler_params=WIDE,
        cost_estimate=cost(0, *outs),
        name="send_scaled",
    )(my_dp, my_hid, ids, weight, *[out_grad] * slices)


def hidden_of(gate, up):
    sig = 1.0 / (1.0 + jnp.exp(-gate))
    return sig, (gate * sig * up).astype(BF16)


def send_kernel(slices, dp_ref, key_ref, gate_ref, up_ref, *o_refs):
    hidden = hidden_of(gate_ref[...].astype(F32), up_ref[...].astype(F32))[1]
    blocks = [block_table(dp_ref[0] ^ k, slices, key_ref[...]) for k in range(len(o_refs))]
    table = ones(jnp.concatenate(blocks, axis=0))
    rows = jnp.dot(table, hidden, preferred_element_type=F32).astype(BF16)
    for k, o_ref in enumerate(o_refs):
        o_ref[...] = rows[k * CAP : (k + 1) * CAP]


def send_hidden(my_dp, slices, slot_key, gate, up):
    slots, depth = gate.shape
    block = 512
    outs = [jax.ShapeDtypeStruct((CAP, depth), BF16)] * (E * slices)
    part = pl.BlockSpec((slots, block), lambda i, d: (0, i))
    return pl.pallas_call(
        functools.partial(send_kernel, slices),
        grid_spec=pltpu.PrefetchScalarGridSpec(
            num_scalar_prefetch=1,
            grid=(depth // block,),
            in_specs=[whole(slot_key), part, part],
            out_specs=[pl.BlockSpec((CAP, block), lambda i, d: (0, i)) for _ in outs],
        ),
        out_shape=outs,
        compiler_params=PARAMS,
        cost_estimate=cost(0, gate, up, *outs),
        name="send_hidden",
    )(my_dp, slot_key, gate, up)


def down_kernel(added, hid_ref, x_ref, w_ref, *refs):
    out = jnp.dot(x_ref[...], w_ref[...], preferred_element_type=F32)
    for a in refs[:added]:
        out = out + a[...].astype(F32)
    o_ref = refs[added]
    o_ref[...] = out.astype(o_ref.dtype)


def down(my_hid, x, weights, q, quarter, dtype, params, *add):
    rows, depth = x.shape
    block = min(512, quarter)
    per = quarter // block
    out = jax.ShapeDtypeStruct((rows, quarter), dtype)
    return pl.pallas_call(
        functools.partial(down_kernel, len(add)),
        grid_spec=pltpu.PrefetchScalarGridSpec(
            num_scalar_prefetch=1,
            grid=(per,),
            in_specs=[
                whole(x),
                pl.BlockSpec((depth, block), lambda j, h: (0, (h[0] ^ q) * per + j)),
            ]
            + [pl.BlockSpec((rows, block), lambda j, h: (0, j)) for _ in add],
            out_specs=pl.BlockSpec((rows, block), lambda j, h: (0, j)),
        ),
        out_shape=out,
        compiler_params=params,
        cost_estimate=cost(
            2 * rows * depth * quarter, x, out, jax.ShapeDtypeStruct((depth, quarter), BF16)
        ),
        name="down",
    )(my_hid, x, weights, *add)


def first_down_kernel(count, per, dp_ref, hid_ref, *refs):
    blocks, w_ref, o_refs, x_ref = refs[:count], refs[count], refs[count + 1 : -1], refs[-1]

    @pl.when(pl.program_id(0) == 0)
    def _():
        for k, b in enumerate(blocks):
            x_ref[rows_of(dp_ref, k), :] = b[...]

    made = jnp.dot(x_ref[...], w_ref[...], preferred_element_type=F32).astype(BF16)
    for i, o_ref in enumerate(o_refs):

        @pl.when(pl.program_id(0) // per == i)
        def _(o_ref=o_ref):
            o_ref[...] = made


def first_down(my_dp, my_hid, blocks, weights, quarters, quarter):
    rows, depth = CAP * len(blocks), blocks[0].shape[1]
    block = min(512, quarter)
    per = quarter // block
    top = quarters[0]
    outs = [jax.ShapeDtypeStruct((rows, quarter), BF16)] * len(quarters)
    outs.append(jax.ShapeDtypeStruct((rows, depth), BF16))

    def place(i):
        return lambda j, d, h: (0, jnp.clip(j - i * per, 0, per - 1))

    return pl.pallas_call(
        functools.partial(first_down_kernel, len(blocks), per),
        grid_spec=pltpu.PrefetchScalarGridSpec(
            num_scalar_prefetch=2,
            grid=(per * len(quarters),),
            in_specs=[whole(b) for b in blocks]
            + [
                pl.BlockSpec(
                    (depth, block),
                    lambda j, d, h: (0, (h[0] ^ (top - 2 * (j // per))) * per + j % per),
                )
            ],
            out_specs=[pl.BlockSpec((rows, block), place(i)) for i in range(len(quarters))]
            + [whole(outs[-1])],
        ),
        out_shape=outs,
        compiler_params=PARAMS,
        cost_estimate=cost(
            2 * rows * depth * quarter, *outs, jax.ShapeDtypeStruct((depth, quarter), BF16)
        ),
        name="first_down",
    )(my_dp, my_hid, *blocks, weights)


def sum_kernel(a_ref, b_ref, o_ref):
    o_ref[...] = (a_ref[...] + b_ref[...].astype(F32)).astype(BF16)


def sum_of(a, b):
    rows, width = a.shape
    block = rows // 2
    part = pl.BlockSpec((block, width), lambda i: (i, 0))
    out = jax.ShapeDtypeStruct((rows, width), BF16)
    return pl.pallas_call(
        sum_kernel,
        grid=(rows // block,),
        in_specs=[part, part],
        out_specs=part,
        out_shape=out,
        compiler_params=WIDE,
        cost_estimate=cost(0, a, b, out),
        name="sum_of",
    )(a, b)


def stack_kernel(*refs):
    *blocks, o_ref = refs
    for k, b in enumerate(blocks):
        o_ref[k * CAP : (k + 1) * CAP, :] = b[...]


def stack(blocks):
    out = jax.ShapeDtypeStruct((CAP * len(blocks), blocks[0].shape[1]), BF16)
    return pl.pallas_call(
        stack_kernel,
        grid=(1,),
        in_specs=[whole(b) for b in blocks],
        out_specs=whole(out),
        out_shape=out,
        compiler_params=PARAMS,
        cost_estimate=cost(0, out, out),
        name="stack",
    )(*blocks)


def rows_of(dp_ref, k):
    return pl.ds(pl.multiple_of((dp_ref[0] ^ k) * CAP, CAP), CAP)


def in_order(dp_ref, halves, y_ref):
    per = halves[0].shape[0] // CAP
    for n, half in enumerate(halves):
        for k in range(per):
            y_ref[n // 2, rows_of(dp_ref, n % 2 * per + k), :] = half[k * CAP : (k + 1) * CAP, :]


def quarter_at(hid_ref, q, quarter):
    return pl.ds(pl.multiple_of((hid_ref[0] ^ q) * quarter, 128), quarter)


def back_kernel(dp_ref, hid_ref, *refs):
    *halves, w_ref, o_ref, y_ref = refs

    @pl.when(pl.program_id(0) == 0)
    def _():
        in_order(dp_ref, halves, y_ref)

    count, _, quarter = y_ref.shape
    total = None
    for q in range(count):
        w = w_ref[:, quarter_at(hid_ref, q, quarter)]
        term = lax.dot_general(y_ref[q], w, COLUMNS, preferred_element_type=F32)
        total = term if total is None else total + term
    o_ref[...] = total.astype(BF16)


def back(my_dp, my_hid, halves, weights):
    rows, quarter = 2 * halves[0].shape[0], halves[0].shape[1]
    depth, width = weights.shape
    block = 256
    out = jax.ShapeDtypeStruct((rows, depth), BF16)
    y = jax.ShapeDtypeStruct((width // quarter, rows, quarter), BF16)
    return pl.pallas_call(
        back_kernel,
        grid_spec=pltpu.PrefetchScalarGridSpec(
            num_scalar_prefetch=2,
            grid=(depth // block,),
            in_specs=[whole(p) for p in halves]
            + [pl.BlockSpec((block, width), lambda i, d, h: (i, 0))],
            out_specs=[pl.BlockSpec((rows, block), lambda i, d, h: (0, i)), whole(y)],
        ),
        out_shape=[out, y],
        compiler_params=PARAMS,
        cost_estimate=cost(2 * rows * depth * width, *halves, weights, out),
        name="back",
    )(my_dp, my_hid, *halves, weights)


def outer_kernel(hid_ref, x_ref, y_ref, o_ref):
    count, _, quarter = y_ref.shape
    x = x_ref[...]
    for q in range(count):
        o_ref[0, :, quarter_at(hid_ref, q, quarter)] = lax.dot_general(
            x, y_ref[q], ROWS, preferred_element_type=F32
        ).astype(BF16)


def outer(my_hid, x, y):
    rows, depth = x.shape
    width = y.shape[0] * y.shape[2]
    block = 256
    out = jax.ShapeDtypeStruct((1, depth, width), BF16)
    return pl.pallas_call(
        outer_kernel,
        grid_spec=pltpu.PrefetchScalarGridSpec(
            num_scalar_prefetch=1,
            grid=(depth // block,),
            in_specs=[pl.BlockSpec((rows, block), lambda i, h: (0, i)), whole(y)],
            out_specs=pl.BlockSpec((1, block, width), lambda i, h: (0, i, 0)),
        ),
        out_shape=out,
        compiler_params=PARAMS,
        cost_estimate=cost(2 * rows * depth * width, x, y, out),
        name="outer",
    )(my_hid, x, y)


def grads_kernel(slices, key_ref, gate_ref, up_ref, back_ref, dgate_ref, dup_ref, dot_ref):
    table = ones(table_of(slices, key_ref[...]))
    h = lax.dot_general(table, back_ref[...], ROWS, preferred_element_type=F32)
    g, u = gate_ref[...].astype(F32), up_ref[...].astype(F32)
    sig, hidden = hidden_of(g, u)
    dgate_ref[...] = (h * u * sig * (1.0 + g * (1.0 - sig))).astype(BF16)
    dup_ref[...] = (h * g * sig).astype(BF16)
    dots = jnp.sum(hidden.astype(F32) * h, axis=1, keepdims=True)

    @pl.when(pl.program_id(0) == 0)
    def _():
        dot_ref[...] = dots

    @pl.when(pl.program_id(0) > 0)
    def _():
        dot_ref[...] += dots


def grads(slices, slot_key, gate, up, got_back):
    slots, depth = gate.shape
    rows = got_back.shape[0]
    block = 512
    part = pl.BlockSpec((slots, block), lambda i: (0, i))
    out = jax.ShapeDtypeStruct(gate.shape, BF16)
    dots = jax.ShapeDtypeStruct((slots, 1), F32)
    return pl.pallas_call(
        functools.partial(grads_kernel, slices),
        grid=(depth // block,),
        in_specs=[
            whole(slot_key),
            part,
            part,
            pl.BlockSpec((rows, block), lambda i: (0, i)),
        ],
        out_specs=[part, part, whole(dots)],
        out_shape=[out, out, dots],
        compiler_params=WIDE,
        cost_estimate=cost(0, gate, up, got_back, out, out),
        name="grads",
    )(slot_key, gate, up, got_back)


def mix_kernel(slices, key_ref, weight_ref, x_ref, *refs):
    o_ref = refs[-1]
    tokens = key_ref.shape[1]
    x = x_ref[...]
    for j in range(slices):
        rows = []
        for d in range(E * slices):
            row = jnp.zeros((CAP, tokens), F32)
            if d % slices == j:
                for s in range(TOP):
                    hit = block_table(d, slices, key_ref[s : s + 1, :])
                    row = jnp.where(hit, weight_ref[s : s + 1, :], row)
            rows.append(row)
        left = jnp.concatenate(rows, axis=0)
        terms = []
        for _ in range(3):
            terms.append(left.astype(BF16))
            left = left - terms[-1].astype(F32)
        sums = lax.dot_general(
            jnp.concatenate(terms, axis=1), x, ROWS, preferred_element_type=F32
        )
        total = sums[:tokens] + sums[tokens : 2 * tokens] + sums[2 * tokens :]
        o_ref[j] = total.astype(BF16)


def mixed_of(slices, slot_key, weight, got_out, after):
    tokens = slot_key.shape[1]
    rows, quarter = got_out.shape
    out = jax.ShapeDtypeStruct((slices, tokens, quarter), BF16)
    return pl.pallas_call(
        functools.partial(mix_kernel, slices),
        grid=(1,),
        in_specs=[whole(slot_key), whole(weight), whole(got_out)]
        + [pl.BlockSpec(memory_space=pl.ANY) for _ in after],
        out_specs=whole(out),
        out_shape=out,
        compiler_params=PARAMS,
        cost_estimate=cost(0, got_out, out),
        name="mixed",
    )(slot_key, weight, got_out, *after)


def per_device(gate_pre, up_pre, out_grad, combine, expert_ids, down_weight):
    dp_count = lax.axis_size("dp")
    hid_count = lax.axis_size("hid")
    my_dp = lax.axis_index("dp").astype(I32).reshape(1)
    my_hid = lax.axis_index("hid").astype(I32).reshape(1)
    slices = dp_count // E
    tokens = gate_pre.shape[0]
    local_ff = gate_pre.shape[2]
    quarter = down_weight.shape[2] // hid_count
    slots = tokens * TOP
    weights = down_weight[0]
    ids, weight = expert_ids.T, combine.T

    def over_dp(x):
        return lax.all_to_all(x, "dp", split_axis=0, concat_axis=0, tiled=True)

    *scaled, slot_key = send_scaled(my_dp, my_hid, ids, weight, out_grad, slices, quarter)
    gate, up = gate_pre.reshape(slots, local_ff), up_pre.reshape(slots, local_ff)
    token_key = slot_key.T.reshape(1, slots)
    hidden = send_hidden(my_dp, slices, token_key, gate, up)

    near, far = list(range(dp_count // 2 - 1, 0, -1)), list(range(dp_count - 1, dp_count // 2 - 1, -1))
    got = {0: scaled[0]}
    for k in far[:2] + near:
        got[k] = swap(scaled[k], "dp", k)
    for k, ahead in zip(far[2:], near * len(far)):
        got[k] = swap(scaled[k], "dp", k, [got[ahead]])
    own = [stack([got[k] for k in part]) for part in ([0, *near[::-1]], far[::-1])]
    own[0] = lax.optimization_barrier((own[0], hidden))[0]
    halves = [{0: x} for x in own]
    bit = hid_count // 2
    for piece in halves:
        piece[bit] = swap(piece[0], "hid", bit)
    halves[0][bit // 2] = swap(own[0], "hid", bit // 2)
    got_hidden = {0: hidden[0]}
    for k, ahead in zip(far[:3], (got[far[2]], got[far[3]], got[far[3]])):
        got_hidden[k] = swap(hidden[k], "dp", k, [ahead])
    while bit > 1:
        bit //= 2
        for piece in halves:
            for q in sorted(piece):
                if q ^ bit not in piece:
                    ahead = [got_hidden[k] for k in far[:2]] if q and piece is halves[1] else []
                    piece[q ^ bit] = swap(piece[q], "hid", bit, ahead)
    got_hidden[near[0]] = swap(hidden[near[0]], "dp", near[0], [halves[1][1]])
    for i, k in enumerate(far[3:] + near[1:]):
        got_hidden[k] = swap(hidden[k], "dp", k, [got_hidden[far[min(i, 1)]]])
    halves = [piece[q] for q in range(hid_count) for piece in halves]
    sent_back, y = back(my_dp, my_hid, halves, weights)
    got_hidden = [got_hidden[k] for k in range(dp_count)]
    got_hidden, sent_back = lax.optimization_barrier((got_hidden, sent_back))

    got_back = over_dp(sent_back)
    others = []
    odd = list(range(hid_count - 1, 0, -2))
    *away, x = first_down(my_dp, my_hid, got_hidden, weights, odd, quarter)
    sums = {q: swap(made, "hid", 1) for q, made in zip(odd, away)}
    for q in range(hid_count - 2, 0, -2):
        made = down(my_hid, x, weights, q, quarter, BF16, PARAMS, sums[q + 1])
        others.append(swap(made, "hid", q))
    x = lax.optimization_barrier((x, made))[0]
    total = down(my_hid, x, weights, 0, quarter, F32, PARAMS, sums[1])
    x = lax.optimization_barrier((x, total))[0]
    weight_grad = outer(my_hid, x, y)
    for other in others[1:]:
        total = total + other.astype(F32)
    total, got_back, weight_grad = lax.optimization_barrier((total, got_back, weight_grad))
    total, got_back = lax.optimization_barrier((sum_of(total, others[0]), got_back))
    got_out = over_dp(total)

    gate_grad, up_grad, dots = grads(slices, token_key, gate, up, got_back)
    shape = (tokens, TOP, local_ff)
    gate_grad, up_grad = gate_grad.reshape(shape), up_grad.reshape(shape)
    cg = dots.reshape(tokens, TOP) / combine
    bit = 1
    while bit < hid_count:
        cg = cg + swap(cg, "hid", bit)
        bit *= 2
    after = (weight_grad, gate_grad, up_grad, cg)
    mixed = mixed_of(slices, slot_key, weight, got_out, after)
    return jnp.swapaxes(mixed, 0, 1), cg, gate_grad, up_grad, weight_grad


def solution(mesh):
    return jax.shard_map(
        per_device,
        mesh=mesh,
        in_specs=(
            P("dp", None, "hid"),
            P("dp", None, "hid"),
            P("dp", None),
            P("dp", None),
            P("dp", None),
            P("dp", "hid", None),
        ),
        out_specs=(
            P("dp", None, "hid"),
            P("dp", None),
            P("dp", None, "hid"),
            P("dp", None, "hid"),
            P("dp", "hid", None),
        ),
        check_vma=False,
    )
```

```python
import functools

import jax
import jax.numpy as jnp
from jax import lax
from jax.experimental import pallas as pl
from jax.experimental.pallas import tpu as pltpu
from jax.sharding import PartitionSpec as P

E = 8
TOP = 2
CAP = 48
F32 = jnp.float32
BF16 = jnp.bfloat16
I32 = jnp.int32
WIDE = pltpu.CompilerParams(vmem_limit_bytes=63 * 1024 * 1024)
PARAMS = pltpu.CompilerParams(vmem_limit_bytes=40 * 1024 * 1024)
ROWS = (((0,), (0,)), ((), ()))
COLUMNS = (((1,), (1,)), ((), ()))
WORK = 1 / 1000


def whole(a):
    return pl.BlockSpec(a.shape, lambda *_: (0,) * len(a.shape))


def cost(flops, *arrays):
    size = sum(a.size * jnp.dtype(a.dtype).itemsize for a in arrays)
    return pl.CostEstimate(
        flops=int(flops * WORK), bytes_accessed=int(size * WORK), transcendentals=0
    )


def swap(x, axis, bit, after=()):
    if len(after):
        x = lax.optimization_barrier((x, tuple(after)))[0]
    count = lax.axis_size(axis)
    return lax.ppermute(x, axis, [(i, i ^ bit) for i in range(count)])


def ones(table):
    return jnp.where(table, 1.0, 0.0).astype(BF16)


def block_table(d, slices, slot_key):
    key = lax.broadcasted_iota(I32, (CAP, slot_key.shape[1]), 0) + d // slices * CAP
    return key == slot_key


def table_of(slices, slot_key):
    count = E * slices
    return jnp.concatenate([block_table(d, slices, slot_key) for d in range(count)], axis=0)


def scale_kernel(slices, dp_ref, hid_ref, ids_ref, weight_ref, *refs):
    grads, o_refs, key_ref = refs[:slices], refs[slices:-1], refs[-1]
    tokens = ids_ref.shape[1]
    slots = tokens * TOP
    ids = jnp.concatenate([ids_ref[s : s + 1] for s in range(TOP)], axis=1)
    weight = jnp.concatenate([weight_ref[s : s + 1] for s in range(TOP)], axis=1)
    is_expert = lax.broadcasted_iota(I32, (E, slots), 0) == ids
    before = lax.broadcasted_iota(I32, (slots, slots), 0) < lax.broadcasted_iota(
        I32, (slots, slots), 1
    )
    earlier = jnp.dot(ones(is_expert), ones(before), preferred_element_type=F32)
    place = jnp.sum(jnp.where(is_expert, earlier, 0.0), axis=0, keepdims=True)
    slot_key = ids * CAP + place.astype(I32)
    for s in range(TOP):
        key_ref[s : s + 1, :] = slot_key[:, s * tokens : (s + 1) * tokens]
    to = [dp_ref[0] ^ k for k in range(E * slices)]
    table = jnp.concatenate([block_table(d, slices, slot_key) for d in to], axis=0)
    row_weight = jnp.sum(jnp.where(table, weight, 0.0), axis=1, keepdims=True)
    picks = ones(table[:, :tokens]) + ones(table[:, tokens:])
    picked = [jnp.dot(picks, g[...], preferred_element_type=F32) for g in grads]
    for k, o_ref in enumerate(o_refs):
        at = slice(k * CAP, (k + 1) * CAP)
        rows = picked[0][at]
        for j in range(1, slices):
            rows = jnp.where(to[k] % slices == j, picked[j][at], rows)
        o_ref[...] = (rows * row_weight[at]).astype(BF16)


def send_scaled(my_dp, my_hid, ids, weight, out_grad, slices, quarter):
    tokens = ids.shape[1]
    hid_count = out_grad.shape[1] // (slices * quarter)
    outs = [jax.ShapeDtypeStruct((CAP, quarter), BF16)] * (E * slices)
    key = jax.ShapeDtypeStruct(ids.shape, I32)

    def part(j):
        return pl.BlockSpec((tokens, quarter), lambda i, d, h: (0, j * hid_count + h[0]))

    return pl.pallas_call(
        functools.partial(scale_kernel, slices),
        grid_spec=pltpu.PrefetchScalarGridSpec(
            num_scalar_prefetch=2,
            grid=(1,),
            in_specs=[whole(ids), whole(weight)] + [part(j) for j in range(slices)],
            out_specs=[whole(o) for o in outs] + [whole(key)],
        ),
        out_shape=outs + [key],
        compiler_params=WIDE,
        cost_estimate=cost(0, *outs),
        name="send_scaled",
    )(my_dp, my_hid, ids, weight, *[out_grad] * slices)


def hidden_of(gate, up):
    sig = 1.0 / (1.0 + jnp.exp(-gate))
    return sig, (gate * sig * up).astype(BF16)


def send_kernel(slices, dp_ref, key_ref, gate_ref, up_ref, *o_refs):
    hidden = hidden_of(gate_ref[...].astype(F32), up_ref[...].astype(F32))[1]
    blocks = [block_table(dp_ref[0] ^ k, slices, key_ref[...]) for k in range(len(o_refs))]
    table = ones(jnp.concatenate(blocks, axis=0))
    rows = jnp.dot(table, hidden, preferred_element_type=F32).astype(BF16)
    for k, o_ref in enumerate(o_refs):
        o_ref[...] = rows[k * CAP : (k + 1) * CAP]


def send_hidden(my_dp, slices, slot_key, gate, up):
    slots, depth = gate.shape
    block = 512
    outs = [jax.ShapeDtypeStruct((CAP, depth), BF16)] * (E * slices)
    part = pl.BlockSpec((slots, block), lambda i, d: (0, i))
    return pl.pallas_call(
        functools.partial(send_kernel, slices),
        grid_spec=pltpu.PrefetchScalarGridSpec(
            num_scalar_prefetch=1,
            grid=(depth // block,),
            in_specs=[whole(slot_key), part, part],
            out_specs=[pl.BlockSpec((CAP, block), lambda i, d: (0, i)) for _ in outs],
        ),
        out_shape=outs,
        compiler_params=PARAMS,
        cost_estimate=cost(0, gate, up, *outs),
        name="send_hidden",
    )(my_dp, slot_key, gate, up)


def down_kernel(added, hid_ref, x_ref, w_ref, *refs):
    out = jnp.dot(x_ref[...], w_ref[...], preferred_element_type=F32)
    for a in refs[:added]:
        out = out + a[...].astype(F32)
    o_ref = refs[added]
    o_ref[...] = out.astype(o_ref.dtype)


def down(my_hid, x, weights, q, quarter, dtype, params, *add):
    rows, depth = x.shape
    block = min(512, quarter)
    per = quarter // block
    out = jax.ShapeDtypeStruct((rows, quarter), dtype)
    return pl.pallas_call(
        functools.partial(down_kernel, len(add)),
        grid_spec=pltpu.PrefetchScalarGridSpec(
            num_scalar_prefetch=1,
            grid=(per,),
            in_specs=[
                whole(x),
                pl.BlockSpec((depth, block), lambda j, h: (0, (h[0] ^ q) * per + j)),
            ]
            + [pl.BlockSpec((rows, block), lambda j, h: (0, j)) for _ in add],
            out_specs=pl.BlockSpec((rows, block), lambda j, h: (0, j)),
        ),
        out_shape=out,
        compiler_params=params,
        cost_estimate=cost(
            2 * rows * depth * quarter, x, out, jax.ShapeDtypeStruct((depth, quarter), BF16)
        ),
        name="down",
    )(my_hid, x, weights, *add)


def first_down_kernel(count, per, dp_ref, hid_ref, *refs):
    blocks, w_ref, o_refs, x_ref = refs[:count], refs[count], refs[count + 1 : -1], refs[-1]

    @pl.when(pl.program_id(0) == 0)
    def _():
        for k, b in enumerate(blocks):
            x_ref[rows_of(dp_ref, k), :] = b[...]

    made = jnp.dot(x_ref[...], w_ref[...], preferred_element_type=F32).astype(BF16)
    for i, o_ref in enumerate(o_refs):

        @pl.when(pl.program_id(0) // per == i)
        def _(o_ref=o_ref):
            o_ref[...] = made


def first_down(my_dp, my_hid, blocks, weights, quarters, quarter):
    rows, depth = CAP * len(blocks), blocks[0].shape[1]
    block = min(512, quarter)
    per = quarter // block
    top = quarters[0]
    outs = [jax.ShapeDtypeStruct((rows, quarter), BF16)] * len(quarters)
    outs.append(jax.ShapeDtypeStruct((rows, depth), BF16))

    def place(i):
        return lambda j, d, h: (0, jnp.clip(j - i * per, 0, per - 1))

    return pl.pallas_call(
        functools.partial(first_down_kernel, len(blocks), per),
        grid_spec=pltpu.PrefetchScalarGridSpec(
            num_scalar_prefetch=2,
            grid=(per * len(quarters),),
            in_specs=[whole(b) for b in blocks]
            + [
                pl.BlockSpec(
                    (depth, block),
                    lambda j, d, h: (0, (h[0] ^ (top - 2 * (j // per))) * per + j % per),
                )
            ],
            out_specs=[pl.BlockSpec((rows, block), place(i)) for i in range(len(quarters))]
            + [whole(outs[-1])],
        ),
        out_shape=outs,
        compiler_params=PARAMS,
        cost_estimate=cost(
            2 * rows * depth * quarter, *outs, jax.ShapeDtypeStruct((depth, quarter), BF16)
        ),
        name="first_down",
    )(my_dp, my_hid, *blocks, weights)


def sum_kernel(a_ref, b_ref, o_ref):
    o_ref[...] = (a_ref[...] + b_ref[...].astype(F32)).astype(BF16)


def sum_of(a, b):
    rows, width = a.shape
    block = rows // 2
    part = pl.BlockSpec((block, width), lambda i: (i, 0))
    out = jax.ShapeDtypeStruct((rows, width), BF16)
    return pl.pallas_call(
        sum_kernel,
        grid=(rows // block,),
        in_specs=[part, part],
        out_specs=part,
        out_shape=out,
        compiler_params=WIDE,
        cost_estimate=cost(0, a, b, out),
        name="sum_of",
    )(a, b)


def stack_kernel(*refs):
    *blocks, o_ref = refs
    for k, b in enumerate(blocks):
        o_ref[k * CAP : (k + 1) * CAP, :] = b[...]


def stack(blocks):
    out = jax.ShapeDtypeStruct((CAP * len(blocks), blocks[0].shape[1]), BF16)
    return pl.pallas_call(
        stack_kernel,
        grid=(1,),
        in_specs=[whole(b) for b in blocks],
        out_specs=whole(out),
        out_shape=out,
        compiler_params=PARAMS,
        cost_estimate=cost(0, out, out),
        name="stack",
    )(*blocks)


def rows_of(dp_ref, k):
    return pl.ds(pl.multiple_of((dp_ref[0] ^ k) * CAP, CAP), CAP)


def in_order(dp_ref, halves, y_ref):
    per = halves[0].shape[0] // CAP
    for n, half in enumerate(halves):
        for k in range(per):
            y_ref[n // 2, rows_of(dp_ref, n % 2 * per + k), :] = half[k * CAP : (k + 1) * CAP, :]


def quarter_at(hid_ref, q, quarter):
    return pl.ds(pl.multiple_of((hid_ref[0] ^ q) * quarter, 128), quarter)


def back_kernel(dp_ref, hid_ref, *refs):
    *halves, w_ref, o_ref, y_ref = refs

    @pl.when(pl.program_id(0) == 0)
    def _():
        in_order(dp_ref, halves, y_ref)

    count, _, quarter = y_ref.shape
    total = None
    for q in range(count):
        w = w_ref[:, quarter_at(hid_ref, q, quarter)]
        term = lax.dot_general(y_ref[q], w, COLUMNS, preferred_element_type=F32)
        total = term if total is None else total + term
    o_ref[...] = total.astype(BF16)


def back(my_dp, my_hid, halves, weights):
    rows, quarter = 2 * halves[0].shape[0], halves[0].shape[1]
    depth, width = weights.shape
    block = 256
    out = jax.ShapeDtypeStruct((rows, depth), BF16)
    y = jax.ShapeDtypeStruct((width // quarter, rows, quarter), BF16)
    return pl.pallas_call(
        back_kernel,
        grid_spec=pltpu.PrefetchScalarGridSpec(
            num_scalar_prefetch=2,
            grid=(depth // block,),
            in_specs=[whole(p) for p in halves]
            + [pl.BlockSpec((block, width), lambda i, d, h: (i, 0))],
            out_specs=[pl.BlockSpec((rows, block), lambda i, d, h: (0, i)), whole(y)],
        ),
        out_shape=[out, y],
        compiler_params=PARAMS,
        cost_estimate=cost(2 * rows * depth * width, *halves, weights, out),
        name="back",
    )(my_dp, my_hid, *halves, weights)


def outer_kernel(hid_ref, x_ref, y_ref, o_ref):
    count, _, quarter = y_ref.shape
    x = x_ref[...]
    for q in range(count):
        o_ref[0, :, quarter_at(hid_ref, q, quarter)] = lax.dot_general(
            x, y_ref[q], ROWS, preferred_element_type=F32
        ).astype(BF16)


def outer(my_hid, x, y):
    rows, depth = x.shape
    width = y.shape[0] * y.shape[2]
    block = 256
    out = jax.ShapeDtypeStruct((1, depth, width), BF16)
    return pl.pallas_call(
        outer_kernel,
        grid_spec=pltpu.PrefetchScalarGridSpec(
            num_scalar_prefetch=1,
            grid=(depth // block,),
            in_specs=[pl.BlockSpec((rows, block), lambda i, h: (0, i)), whole(y)],
            out_specs=pl.BlockSpec((1, block, width), lambda i, h: (0, i, 0)),
        ),
        out_shape=out,
        compiler_params=PARAMS,
        cost_estimate=cost(2 * rows * depth * width, x, y, out),
        name="outer",
    )(my_hid, x, y)


def grads_kernel(slices, key_ref, gate_ref, up_ref, back_ref, dgate_ref, dup_ref, dot_ref):
    table = ones(table_of(slices, key_ref[...]))
    h = lax.dot_general(table, back_ref[...], ROWS, preferred_element_type=F32)
    g, u = gate_ref[...].astype(F32), up_ref[...].astype(F32)
    sig, hidden = hidden_of(g, u)
    dgate_ref[...] = (h * u * sig * (1.0 + g * (1.0 - sig))).astype(BF16)
    dup_ref[...] = (h * g * sig).astype(BF16)
    dots = jnp.sum(hidden.astype(F32) * h, axis=1, keepdims=True)

    @pl.when(pl.program_id(0) == 0)
    def _():
        dot_ref[...] = dots

    @pl.when(pl.program_id(0) > 0)
    def _():
        dot_ref[...] += dots


def grads(slices, slot_key, gate, up, got_back):
    slots, depth = gate.shape
    rows = got_back.shape[0]
    block = 512
    part = pl.BlockSpec((slots, block), lambda i: (0, i))
    out = jax.ShapeDtypeStruct(gate.shape, BF16)
    dots = jax.ShapeDtypeStruct((slots, 1), F32)
    return pl.pallas_call(
        functools.partial(grads_kernel, slices),
        grid=(depth // block,),
        in_specs=[
            whole(slot_key),
            part,
            part,
            pl.BlockSpec((rows, block), lambda i: (0, i)),
        ],
        out_specs=[part, part, whole(dots)],
        out_shape=[out, out, dots],
        compiler_params=WIDE,
        cost_estimate=cost(0, gate, up, got_back, out, out),
        name="grads",
    )(slot_key, gate, up, got_back)


def mix_kernel(slices, key_ref, weight_ref, x_ref, *refs):
    o_ref = refs[-1]
    tokens = key_ref.shape[1]
    x = x_ref[...]
    for j in range(slices):
        rows = []
        for d in range(E * slices):
            row = jnp.zeros((CAP, tokens), F32)
            if d % slices == j:
                for s in range(TOP):
                    hit = block_table(d, slices, key_ref[s : s + 1, :])
                    row = jnp.where(hit, weight_ref[s : s + 1, :], row)
            rows.append(row)
        left = jnp.concatenate(rows, axis=0)
        terms = []
        for _ in range(3):
            terms.append(left.astype(BF16))
            left = left - terms[-1].astype(F32)
        sums = lax.dot_general(
            jnp.concatenate(terms, axis=1), x, ROWS, preferred_element_type=F32
        )
        total = sums[:tokens] + sums[tokens : 2 * tokens] + sums[2 * tokens :]
        o_ref[j] = total.astype(BF16)


def mixed_of(slices, slot_key, weight, got_out, after):
    tokens = slot_key.shape[1]
    rows, quarter = got_out.shape
    out = jax.ShapeDtypeStruct((slices, tokens, quarter), BF16)
    return pl.pallas_call(
        functools.partial(mix_kernel, slices),
        grid=(1,),
        in_specs=[whole(slot_key), whole(weight), whole(got_out)]
        + [pl.BlockSpec(memory_space=pl.ANY) for _ in after],
        out_specs=whole(out),
        out_shape=out,
        compiler_params=PARAMS,
        cost_estimate=cost(0, got_out, out),
        name="mixed",
    )(slot_key, weight, got_out, *after)


def per_device(gate_pre, up_pre, out_grad, combine, expert_ids, down_weight):
    dp_count = lax.axis_size("dp")
    hid_count = lax.axis_size("hid")
    my_dp = lax.axis_index("dp").astype(I32).reshape(1)
    my_hid = lax.axis_index("hid").astype(I32).reshape(1)
    slices = dp_count // E
    tokens = gate_pre.shape[0]
    local_ff = gate_pre.shape[2]
    quarter = down_weight.shape[2] // hid_count
    slots = tokens * TOP
    weights = down_weight[0]
    ids, weight = expert_ids.T, combine.T

    def over_dp(x):
        return lax.all_to_all(x, "dp", split_axis=0, concat_axis=0, tiled=True)

    *scaled, slot_key = send_scaled(my_dp, my_hid, ids, weight, out_grad, slices, quarter)
    gate, up = gate_pre.reshape(slots, local_ff), up_pre.reshape(slots, local_ff)
    token_key = slot_key.T.reshape(1, slots)
    hidden = send_hidden(my_dp, slices, token_key, gate, up)

    near, far = list(range(dp_count // 2 - 1, 0, -1)), list(range(dp_count - 1, dp_count // 2 - 1, -1))
    got = {0: scaled[0]}
    for k in far[:2] + near:
        got[k] = swap(scaled[k], "dp", k)
    for k, ahead in zip(far[2:], near * len(far)):
        got[k] = swap(scaled[k], "dp", k, [got[ahead]])
    own = [stack([got[k] for k in part]) for part in ([0, *near[::-1]], far[::-1])]
    own[0] = lax.optimization_barrier((own[0], hidden))[0]
    halves = [{0: x} for x in own]
    bit = hid_count // 2
    for piece in halves:
        piece[bit] = swap(piece[0], "hid", bit)
    halves[0][bit // 2] = swap(own[0], "hid", bit // 2)
    got_hidden = {0: hidden[0]}
    for k, ahead in zip(far[:3], (got[far[2]], got[far[3]], got[far[3]])):
        got_hidden[k] = swap(hidden[k], "dp", k, [ahead])
    while bit > 1:
        bit //= 2
        for piece in halves:
            for q in sorted(piece):
                if q ^ bit not in piece:
                    ahead = [got_hidden[k] for k in far[:2]] if q and piece is halves[1] else []
                    piece[q ^ bit] = swap(piece[q], "hid", bit, ahead)
    got_hidden[near[0]] = swap(hidden[near[0]], "dp", near[0], [halves[1][1]])
    for i, k in enumerate(far[3:] + near[1:]):
        got_hidden[k] = swap(hidden[k], "dp", k, [got_hidden[far[min(i, 1)]]])
    halves = [piece[q] for q in range(hid_count) for piece in halves]
    sent_back, y = back(my_dp, my_hid, halves, weights)
    got_hidden = [got_hidden[k] for k in range(dp_count)]
    got_hidden, sent_back = lax.optimization_barrier((got_hidden, sent_back))

    got_back = over_dp(sent_back)
    others = []
    odd = list(range(hid_count - 1, 0, -2))
    made, x = first_down(my_dp, my_hid, got_hidden, weights, odd[:1], quarter)
    sums = {odd[0]: swap(made, "hid", 1)}
    for q in odd[1:]:
        made = down(my_hid, x, weights, q, quarter, BF16, PARAMS)
        sums[q] = swap(made, "hid", 1)
    x = lax.optimization_barrier((x, made))[0]
    for q in range(hid_count - 2, 0, -2):
        made = down(my_hid, x, weights, q, quarter, BF16, PARAMS, sums[q + 1])
        others.append(swap(made, "hid", q))
    x = lax.optimization_barrier((x, made))[0]
    total = down(my_hid, x, weights, 0, quarter, F32, PARAMS, sums[1])
    x = lax.optimization_barrier((x, total))[0]
    weight_grad = outer(my_hid, x, y)
    for other in others[1:]:
        total = total + other.astype(F32)
    total, got_back, weight_grad = lax.optimization_barrier((total, got_back, weight_grad))
    total, got_back = lax.optimization_barrier((sum_of(total, others[0]), got_back))
    got_out = over_dp(total)

    gate_grad, up_grad, dots = grads(slices, token_key, gate, up, got_back)
    shape = (tokens, TOP, local_ff)
    gate_grad, up_grad = gate_grad.reshape(shape), up_grad.reshape(shape)
    cg = dots.reshape(tokens, TOP) / combine
    bit = 1
    while bit < hid_count:
        cg = cg + swap(cg, "hid", bit)
        bit *= 2
    after = (weight_grad, gate_grad, up_grad, cg)
    mixed = mixed_of(slices, slot_key, weight, got_out, after)
    return jnp.swapaxes(mixed, 0, 1), cg, gate_grad, up_grad, weight_grad


def solution(mesh):
    return jax.shard_map(
        per_device,
        mesh=mesh,
        in_specs=(
            P("dp", None, "hid"),
            P("dp", None, "hid"),
            P("dp", None),
            P("dp", None),
            P("dp", None),
            P("dp", "hid", None),
        ),
        out_specs=(
            P("dp", None, "hid"),
            P("dp", None),
            P("dp", None, "hid"),
            P("dp", None, "hid"),
            P("dp", "hid", None),
        ),
        check_vma=False,
    )
```
